512 devices in a mesh: seq: 32 (over x, y_lo, core), res: 16 (over y_hi, z).
Axes of the slice: x: 4, y: 8 (y_hi: 2, y_lo: 4; y = y_hi * 4 + y_lo), z: 8, core: 2. Of those that a mesh axis runs over, the one named last changes fastest.
Arguments:
- alignment: bfloat16 [256, 512, 768], P('seq', 'res'), may hold values from -6 to 6
- row_gain: bfloat16 [768], replicated, may hold values from 0.099609375 to 1.8984375
- row_project: bfloat16 [768, 1152], replicated, may hold values from -4 to 4
- row_output: bfloat16 [384, 768], replicated, may hold values from -2.5 to 2.5
- column_gain: bfloat16 [768], replicated, may hold values from 0.099609375 to 1.8984375
- column_project: bfloat16 [768, 1152], replicated, may hold values from -4 to 4
Outputs:
- row_updated: bfloat16 [256, 512, 768], P('seq', 'res')
- column_context: bfloat16 [256, 512, 384], P('seq', 'res')
The draws below stay inside these ranges and needn't reach their ends.
All inputs are finite; a program needn't handle non-finite values.
Results may differ from the reference program's by a relative error of at most 0.025.
Values may be sent and summed in bfloat16 or wider, within the bound.
A program may use at most 64 MiB of HBM per device.

```python
import math
import jax
import jax.numpy as jnp
from jax import lax

D = 768
HEADS = 6
HEAD = 64
COL_DEV = 32
ROWS = 256
COLS = 512
N_RES = 16


def projection(key):
    first = jax.random.fold_in(key, 0)
    base = jax.random.normal(first, (D, 3, HEADS, HEAD), jnp.float32) * D ** (-0.5)
    keys_part = base[:, 1]
    stacked = jnp.stack([base[:, 0], keys_part, base[:, 2]], axis=1)
    return jnp.clip(stacked, -4.0, 4.0).reshape(D, 3 * HEADS * HEAD).astype(jnp.bfloat16)


def draw_alignment(key, part):
    key = jax.random.fold_in(key, 11)
    first = jax.random.fold_in(key, 0)
    values = jnp.clip(jax.random.normal(first, (ROWS, COLS, D), jnp.float32), -6.0, 6.0)
    return values.astype(jnp.bfloat16)


def draw_row_project(key, part):
    key = jax.random.fold_in(key, 12)
    return projection(key)


def draw_column_project(key, part):
    key = jax.random.fold_in(key, 13)
    return projection(key)


def scatter_about(own_key, extent, deviation, most, dtype=jnp.bfloat16):
    result = jax.random.normal(own_key, extent, jnp.float32) * deviation
    return jnp.minimum(jnp.maximum(result, -most), most).astype(dtype)


def setup_inputs(seed: int = 0) -> dict:
    streams_of = jax.random.split(jax.random.key(seed), 7)
    return {
        "alignment": draw_alignment(jax.random.fold_in(streams_of[6], 71), 0),
        "row_gain": jnp.clip(1.0 + 0.18 * jax.random.normal(streams_of[1], (D,), jnp.float32), 0.099609375, 1.8984375).astype(jnp.bfloat16),
        "row_project": draw_row_project(jax.random.fold_in(streams_of[6], 71), 0),
        "row_output": scatter_about(streams_of[3], (HEADS * HEAD, D), (HEADS * HEAD // 64) ** -0.5, 2.5),
        "column_gain": jnp.clip(1.0 + 0.18 * jax.random.normal(streams_of[4], (D,), jnp.float32), 0.099609375, 1.8984375).astype(jnp.bfloat16),
        "column_project": draw_column_project(jax.random.fold_in(streams_of[6], 71), 0),
    }


def layer_norm(values, gain):
    average = lax.optimization_barrier(jnp.mean(values, axis=-1, keepdims=True))
    centred = values - average
    spread = lax.optimization_barrier(jnp.mean(centred * centred, axis=-1, keepdims=True))
    return centred * lax.rsqrt(spread + 1e-05) * gain.astype(jnp.float32)

def widen(values):
    return lax.optimization_barrier(values).astype(jnp.float32)

def reference(alignment, row_gain, row_project, row_output, column_gain, column_project):
    inner = HEADS * HEAD
    source = alignment.astype(jnp.float32)
    normed = layer_norm(source, row_gain).astype(jnp.bfloat16)
    packed = jnp.dot(normed.reshape(ROWS * COLS, D), row_project, preferred_element_type=jnp.float32).astype(jnp.bfloat16)
    packed = widen(packed).reshape(ROWS, COLS, 3, HEADS, HEAD)
    queries = packed[:, :, 0]
    keys_all = packed[:, :, 1]
    values_all = packed[:, :, 2]
    scaling = 1.0 / (math.sqrt(HEAD) * math.sqrt(ROWS))
    logits = jnp.einsum('rihe,rjhe->hij', queries, keys_all) * scaling
    tied = widen(jax.nn.softmax(logits, axis=-1).astype(jnp.bfloat16))
    context = jnp.einsum('hij,rjhe->rihe', tied, values_all).astype(jnp.bfloat16)
    update = jnp.dot(context.reshape(ROWS * COLS, inner), row_output, preferred_element_type=jnp.float32)
    row_updated = (source + update.reshape(ROWS, COLS, D)).astype(jnp.bfloat16)
    normed_col = layer_norm(widen(row_updated), column_gain).astype(jnp.bfloat16)
    packed_col = jnp.dot(normed_col.reshape(ROWS * COLS, D), column_project, preferred_element_type=jnp.float32).astype(jnp.bfloat16)
    packed_col = widen(packed_col).reshape(ROWS, N_RES, COL_DEV, 3, HEADS, HEAD)
    packed_col = jnp.transpose(packed_col, (1, 0, 2, 3, 4, 5))

    def column_block(block):
        scores = jnp.einsum('rche,sche->chrs', block[:, :, 0], block[:, :, 1]) / math.sqrt(HEAD)
        weights = widen(jax.nn.softmax(scores, axis=-1).astype(jnp.bfloat16))
        return jnp.einsum('chrs,sche->rche', weights, block[:, :, 2]).astype(jnp.bfloat16)
    blocks = lax.map(column_block, packed_col)
    column_context = jnp.transpose(blocks, (1, 0, 2, 3, 4)).reshape(ROWS, COLS, inner)
    return (row_updated, column_context)
```

```python
import functools
import math

import jax
import jax.numpy as jnp
from jax import lax
from jax.experimental import pallas as pl
from jax.experimental.pallas import tpu as pltpu
from jax.sharding import PartitionSpec as P

HEADS = 6
HEAD = 64
INNER = HEADS * HEAD
LANES = 128
Z = 8
MESH = pl.DeviceIdType.MESH


def layer_norm(values, gain):
    average = jnp.mean(values, axis=-1, keepdims=True)
    centred = values - average
    spread = jnp.mean(centred * centred, axis=-1, keepdims=True)
    return centred * lax.rsqrt(spread + 1e-05) * gain.astype(jnp.float32)


def low_lanes(shape):
    return lax.broadcasted_iota(jnp.int32, shape, len(shape) - 1) < HEAD


def arrived(ref, sem):
    pltpu.make_async_copy(ref, ref, sem).wait()


def kernel(
    seqs, x_ref, g1_ref, w1_ref, g2_ref, wo_hbm, w2_hbm, ru_ref, cc_ref,
    wo_ref, w2_ref, tiles, rq, rk, rv, lp, rl, td, rt, oc, rc, pc, rp, ac, ra,
    load_sem, out_q, out_k, out_v, in_qkv, out_c, in_c, out_seq, in_seq,
):
    rows, cols, features = x_ref.shape
    tokens = rows * cols
    half = tokens // 2
    res = 2 * Z
    here = Z * cols
    everywhere = res * cols
    share = here // seqs
    per_device = cols // seqs
    f32, bf16 = jnp.float32, jnp.bfloat16

    s = lax.axis_index("seq")
    t = lax.axis_index("res")
    yh = t // Z
    z = t % Z
    worker = z % 4 != 3
    head_here = z - z // 4

    barrier = pltpu.get_barrier_semaphore()

    def greet_seq(k, carry):
        pl.semaphore_signal(barrier, inc=1, device_id={"seq": lax.rem(s + k, seqs)}, device_id_type=MESH)
        return carry

    def greet_res(k, carry):
        pl.semaphore_signal(barrier, inc=1, device_id={"res": lax.rem(t + k, res)}, device_id_type=MESH)
        return carry

    lax.fori_loop(1, seqs, greet_seq, 0)
    lax.fori_loop(1, res, greet_res, 0)

    load_wo = pltpu.make_async_copy(wo_hbm, wo_ref, load_sem.at[0])
    load_w2 = pltpu.make_async_copy(w2_hbm, w2_ref, load_sem.at[1])
    load_wo.start()
    load_w2.start()

    source = x_ref[...].reshape(tokens, features).astype(f32)
    normed = layer_norm(source, g1_ref[...]).astype(bf16)

    def project(part):
        packed = jnp.dot(normed, w1_ref[:, part * INNER : (part + 1) * INNER], preferred_element_type=f32)
        for pair in range(HEADS // 2):
            tile = packed[:, pair * LANES : (pair + 1) * LANES]
            turned = pltpu.roll(tile, HEAD, 1)
            low = low_lanes((half, LANES))
            first = jnp.where(low, tile[:half], turned[half:]).astype(bf16)
            second = jnp.where(low, turned[:half], tile[half:]).astype(bf16)
            tiles[part, 2 * pair] = first.reshape(rows // 2, cols, LANES)
            tiles[part, 2 * pair + 1] = second.reshape(rows // 2, cols, LANES)

    def send_head(part, dst, slot, send, recv, both):
        def step(h, carry):
            at = h + h // 3
            block = tiles.at[part, h]

            @pl.when(z == at)
            def _():
                pltpu.make_async_copy(block, dst.at[slot], recv).start()

            @pl.when(z != at)
            def _():
                pltpu.make_async_remote_copy(
                    block, dst.at[slot], send.at[h, 0], recv,
                    device_id={"res": yh * Z + at}, device_id_type=MESH,
                ).start()

            if both:
                pltpu.make_async_remote_copy(
                    block, dst.at[slot], send.at[h, 1], recv,
                    device_id={"res": (1 - yh) * Z + at}, device_id_type=MESH,
                ).start()
            return carry

        lax.fori_loop(0, HEADS, step, 0)

    def sent_head(part, send, both):
        def step(h, carry):
            at = h + h // 3
            block = tiles.at[part, h]

            @pl.when(z != at)
            def _():
                arrived(block, send.at[h, 0])

            if both:
                arrived(block, send.at[h, 1])
            return carry

        lax.fori_loop(0, HEADS, step, 0)

    def exchange(block, dst, stage):
        pltpu.make_async_copy(block(s), dst.at[s], in_seq.at[stage]).start()

        def step(k, carry):
            peer = lax.rem(s + k, seqs)
            pltpu.make_async_remote_copy(
                block(peer), dst.at[s], out_seq.at[stage], in_seq.at[stage],
                device_id={"seq": peer}, device_id_type=MESH,
            ).start()
            return carry

        lax.fori_loop(1, seqs, step, 0)

    def sent(dst, stage):
        arrived(dst.at[pl.ds(0, seqs - 1)], out_seq.at[stage])

    project(1)
    pl.semaphore_wait(barrier, seqs + res - 2)
    send_head(1, rk, t, out_k, in_qkv.at[1], True)
    project(0)
    send_head(0, rq, z, out_q, in_qkv.at[0], False)
    project(2)
    send_head(2, rv, t, out_v, in_qkv.at[2], True)

    @pl.when(worker)
    def _():
        arrived(rk, in_qkv.at[1])
        arrived(rq, in_qkv.at[0])
        quads = rows // 2
        queries = jnp.concatenate([rq[:, r].reshape(here, LANES) for r in range(quads)], axis=1)
        keys = jnp.concatenate([rk[:, r].reshape(everywhere, LANES) for r in range(quads)], axis=1)
        logits = lax.dot_general(
            queries, keys, (((1,), (1,)), ((), ())), preferred_element_type=f32
        ) * (1.0 / (math.sqrt(HEAD) * math.sqrt(rows * seqs)))
        logits = logits.reshape(seqs, share, everywhere)
        lp[...] = jnp.concatenate([logits[:, :, :here], logits[:, :, here:]], axis=1).astype(bf16)
        exchange(lambda peer: lp.at[peer], rl, 0)
        arrived(rl, in_seq.at[0])
        total = jnp.sum(rl[...].astype(f32), axis=0)
        left, right = total[:share], total[share:]
        most = jnp.maximum(
            jnp.max(left, axis=-1, keepdims=True), jnp.max(right, axis=-1, keepdims=True)
        )
        left, right = jnp.exp(left - most), jnp.exp(right - most)
        norm = jnp.sum(left, axis=-1, keepdims=True) + jnp.sum(right, axis=-1, keepdims=True)
        td[...] = jnp.concatenate([left / norm, right / norm], axis=0).astype(bf16)
        exchange(lambda peer: td, rt, 1)
        arrived(rv, in_qkv.at[2])
        values = jnp.concatenate([rv[:, r].reshape(everywhere, LANES) for r in range(quads)], axis=1)
        arrived(rt, in_seq.at[1])
        tied = rt[...].astype(f32)
        left = tied[:, :share].reshape(here, here).astype(bf16)
        right = tied[:, share:].reshape(here, here).astype(bf16)
        context = jnp.dot(left, values[:here], preferred_element_type=f32)
        context += jnp.dot(right, values[here:], preferred_element_type=f32)
        for r in range(quads):
            oc[:, r] = context[:, r * LANES : (r + 1) * LANES].reshape(Z, cols, LANES).astype(bf16)
        pltpu.make_async_copy(oc.at[z], rc.at[head_here], in_c).start()

        def step(k, carry):
            peer = lax.rem(z + k, Z)
            pltpu.make_async_remote_copy(
                oc.at[peer], rc.at[head_here], out_c, in_c,
                device_id={"res": yh * Z + peer}, device_id_type=MESH,
            ).start()
            return carry

        lax.fori_loop(1, Z, step, 0)

    load_wo.wait()
    load_w2.wait()
    arrived(rc, in_c)
    low = low_lanes((half, LANES))
    tops, bottoms = [], []
    for pair in range(HEADS // 2):
        first = rc[2 * pair].reshape(half, LANES).astype(f32)
        second = rc[2 * pair + 1].reshape(half, LANES).astype(f32)
        tops.append(jnp.where(low, first, pltpu.roll(second, HEAD, 1)).astype(bf16))
        bottoms.append(jnp.where(low, pltpu.roll(first, HEAD, 1), second).astype(bf16))
    context = jnp.concatenate(
        [jnp.concatenate(tops, axis=1), jnp.concatenate(bottoms, axis=1)], axis=0
    )
    update = jnp.dot(context, wo_ref[...], preferred_element_type=f32)
    source = x_ref[...].reshape(tokens, features).astype(f32)
    row_updated = (source + update).astype(bf16)
    ru_ref[...] = row_updated.reshape(rows, cols, features)
    normed = layer_norm(row_updated.astype(f32), g2_ref[...]).astype(bf16)
    one = lax.broadcasted_iota(jnp.int32, (tokens, tokens), 0)
    two = lax.broadcasted_iota(jnp.int32, (tokens, tokens), 1)
    turn = jnp.where((one % rows) * cols + one // rows == two, 1.0, 0.0).astype(bf16)
    normed = jnp.dot(turn, normed, preferred_element_type=f32).astype(bf16)
    for part in range(3):
        span = slice(part * INNER, (part + 1) * INNER)
        packed = jnp.dot(normed, w2_ref[:, span], preferred_element_type=f32).astype(bf16)
        pc[:, :, :, span] = packed.reshape(seqs, per_device, rows, INNER)
    exchange(lambda peer: pc.at[peer], rp, 2)
    arrived(rp, in_seq.at[2])
    total_rows = seqs * rows
    low = low_lanes((total_rows, LANES))
    zero = jnp.zeros((total_rows, LANES), bf16)
    for c in range(per_device):
        for pair in range(HEADS // 2):
            span = slice(pair * LANES, (pair + 1) * LANES)
            query, key, value = (
                rp[:, c, :, part * INNER + pair * LANES : part * INNER + (pair + 1) * LANES].reshape(total_rows, LANES)
                for part in range(3)
            )
            mixed = []
            for mask in (low, jnp.logical_not(low)):
                scores = lax.dot_general(
                    jnp.where(mask, query, zero), key, (((1,), (1,)), ((), ())), preferred_element_type=f32
                ) * (1.0 / math.sqrt(HEAD))
                scores = jnp.exp(scores - jnp.max(scores, axis=-1, keepdims=True))
                weights = (scores / jnp.sum(scores, axis=-1, keepdims=True)).astype(bf16)
                mixed.append(jnp.dot(weights, value, preferred_element_type=f32))
            ac[:, c, :, span] = jnp.where(low, mixed[0], mixed[1]).astype(bf16).reshape(seqs, rows, LANES)
    exchange(lambda peer: ac.at[peer], ra, 3)
    back = jnp.where((two % rows) * cols + two // rows == one, 1.0, 0.0).astype(bf16)
    arrived(ra, in_seq.at[3])
    result = jnp.dot(back, ra[...].reshape(tokens, INNER), preferred_element_type=f32).astype(bf16)
    cc_ref[...] = result.reshape(rows, cols, INNER)

    sent_head(1, out_k, True)
    sent_head(0, out_q, False)
    sent_head(2, out_v, True)

    @pl.when(worker)
    def _():
        sent(rl, 0)
        sent(rt, 1)
        arrived(oc.at[pl.ds(0, Z - 1)], out_c)

    sent(rp, 2)
    sent(ra, 3)


def body(seqs, alignment, row_gain, row_project, row_output, column_gain, column_project):
    rows, cols, features = alignment.shape
    res = 2 * Z
    here = Z * cols
    share = here // seqs
    per_device = cols // seqs
    bf16 = jnp.bfloat16
    vmem = pl.BlockSpec(memory_space=pltpu.VMEM)
    hbm = pl.BlockSpec(memory_space=pl.ANY)
    head = (rows // 2, cols, LANES)
    dma = pltpu.SemaphoreType.DMA
    return pl.pallas_call(
        functools.partial(kernel, seqs),
        out_shape=(
            jax.ShapeDtypeStruct((rows, cols, features), bf16),
            jax.ShapeDtypeStruct((rows, cols, INNER), bf16),
        ),
        in_specs=[vmem, vmem, vmem, vmem, hbm, hbm],
        out_specs=(vmem, vmem),
        scratch_shapes=[
            pltpu.VMEM(row_output.shape, bf16),
            pltpu.VMEM(column_project.shape, bf16),
            pltpu.VMEM((3, HEADS) + head, bf16),
            pltpu.VMEM((Z,) + head, bf16),
            pltpu.VMEM((res,) + head, bf16),
            pltpu.VMEM((res,) + head, bf16),
            pltpu.VMEM((seqs, 2 * share, here), bf16),
            pltpu.VMEM((seqs, 2 * share, here), bf16),
            pltpu.VMEM((2 * share, here), bf16),
            pltpu.VMEM((seqs, 2 * share, here), bf16),
            pltpu.VMEM((Z,) + head, bf16),
            pltpu.VMEM((HEADS,) + head, bf16),
            pltpu.VMEM((seqs, per_device, rows, 3 * INNER), bf16),
            pltpu.VMEM((seqs, per_device, rows, 3 * INNER), bf16),
            pltpu.VMEM((seqs, per_device, rows, INNER), bf16),
            pltpu.VMEM((seqs, per_device, rows, INNER), bf16),
            dma((2,)),
            dma((HEADS, 1)),
            dma((HEADS, 2)),
            dma((HEADS, 2)),
            dma((3,)),
            dma,
            dma,
            dma((4,)),
            dma((4,)),
        ],
        compiler_params=pltpu.CompilerParams(
            collective_id=0, has_side_effects=True, vmem_limit_bytes=40 * 1024 * 1024
        ),
        name="msa_layer",
    )(
        alignment, row_gain.reshape(1, features), row_project,
        column_gain.reshape(1, features), row_output, column_project,
    )


def solution(mesh):
    placed = (P("seq", "res", None), P(), P(), P(), P(), P())
    return jax.shard_map(
        functools.partial(body, mesh.shape["seq"]),
        mesh=mesh,
        in_specs=placed,
        out_specs=(P("seq", "res", None), P("seq", "res", None)),
        check_vma=False,
    )
```

```python
import functools
import math

import jax
import jax.numpy as jnp
from jax import lax
from jax.experimental import pallas as pl
from jax.experimental.pallas import tpu as pltpu
from jax.sharding import PartitionSpec as P

HEADS = 6
HEAD = 64
INNER = HEADS * HEAD
LANES = 128
Z = 8
CORES = 2
FAR_FIRST = (4, 3, 5, 2, 6, 1, 7, 0)
MESH = pl.DeviceIdType.MESH


def layer_norm(values, gain):
    average = jnp.mean(values, axis=-1, keepdims=True)
    centred = values - average
    spread = jnp.mean(centred * centred, axis=-1, keepdims=True)
    return centred * lax.rsqrt(spread + 1e-05) * gain.astype(jnp.float32)


def low_lanes(shape):
    return lax.broadcasted_iota(jnp.int32, shape, len(shape) - 1) < HEAD


def arrived(ref, sem):
    pltpu.make_async_copy(ref, ref, sem).wait()


def kernel(
    seqs, x_hbm, g1_ref, w1_hbm, g2_ref, wo_hbm, w2_hbm, ru_ref, cc_ref,
    x_ref, w1_ref, wo_ref, w2_ref, tiles, rq, rk, rv, lp, rl, l2, r2, td, rd, t4, rt, oc, rc,
    xs, rx, cs, rcs, ac, ra,
    load_sem, out_q, out_k, out_v, in_q, in_k, in_v, out_c, in_c, out_seq, in_seq,
):
    rows, cols, features = x_ref.shape
    tokens = rows * cols
    half = tokens // 2
    quads = rows // 2
    res = 2 * Z
    here = Z * cols
    everywhere = res * cols
    per_device = cols // seqs
    n_b = min(4, seqs // CORES)
    n_a = seqs // n_b
    f32, bf16 = jnp.float32, jnp.bfloat16

    s = lax.axis_index("seq")
    t = lax.axis_index("res")
    yh = t // Z
    z = t % Z
    worker = z % 4 != 3
    head_here = z - z // 4
    core = s % CORES
    b = (s // CORES) % n_b
    a = s // (CORES * n_b) * CORES + core

    def a_peer(k):
        return (k // CORES) * (CORES * n_b) + b * CORES + k % CORES

    def b_peer(k):
        return (a // CORES) * (CORES * n_b) + k * CORES + core

    def s_peer(k):
        return k

    loads = [
        pltpu.make_async_copy(src, dst, load_sem.at[i])
        for i, (src, dst) in enumerate(
            ((x_hbm, x_ref), (w1_hbm, w1_ref), (wo_hbm, wo_ref), (w2_hbm, w2_ref))
        )
    ]
    for load in loads:
        load.start()

    barrier = pltpu.get_barrier_semaphore()

    def greet_seq(k, carry):
        pl.semaphore_signal(barrier, inc=1, device_id={"seq": lax.rem(s + k, seqs)}, device_id_type=MESH)
        return carry

    def greet_res(k, carry):
        pl.semaphore_signal(barrier, inc=1, device_id={"res": lax.rem(t + k, res)}, device_id_type=MESH)
        return carry

    lax.fori_loop(1, res, greet_res, 0)
    lax.fori_loop(1, seqs, greet_seq, 0)

    loads[0].wait()
    source = x_ref[...].reshape(tokens, features).astype(f32)
    normed = layer_norm(source, g1_ref[...].reshape(1, features)).astype(bf16)
    loads[1].wait()

    def project(part):
        packed = jnp.dot(normed, w1_ref[:, part * INNER : (part + 1) * INNER], preferred_element_type=f32)
        for pair in range(HEADS // 2):
            tile = packed[:, pair * LANES : (pair + 1) * LANES]
            turned = pltpu.roll(tile, HEAD, 1)
            low = low_lanes((half, LANES))
            first = jnp.where(low, tile[:half], turned[half:]).astype(bf16)
            second = jnp.where(low, turned[:half], tile[half:]).astype(bf16)
            tiles[part, 2 * pair] = first.reshape(quads, cols, LANES)
            tiles[part, 2 * pair + 1] = second.reshape(quads, cols, LANES)

    def send_head(part, dst, slot, send, recv, both, offsets=FAR_FIRST):
        for offset in offsets:
            at = lax.rem(z + offset, Z)

            @pl.when(at % 4 != 3)
            def _():
                h = at - at // 4
                block = tiles.at[part, h]
                if offset == 0:
                    pltpu.make_async_copy(block, dst.at[slot], recv).start()
                else:
                    pltpu.make_async_remote_copy(
                        block, dst.at[slot], send.at[h, 0], recv,
                        device_id={"res": yh * Z + at}, device_id_type=MESH,
                    ).start()
                if both:
                    pltpu.make_async_remote_copy(
                        block, dst.at[slot], send.at[h, 1], recv,
                        device_id={"res": (1 - yh) * Z + at}, device_id_type=MESH,
                    ).start()

    def sent_head(part, send, both):
        def step(h, carry):
            at = h + h // 3
            block = tiles.at[part, h]

            @pl.when(z != at)
            def _():
                arrived(block, send.at[h, 0])

            if both:
                arrived(block, send.at[h, 1])
            return carry

        lax.fori_loop(0, HEADS, step, 0)

    def exchange(block, dst, stage, me, count, peer_of):
        pltpu.make_async_copy(block(me), dst.at[me], in_seq.at[stage]).start()

        def step(k, carry):
            peer = lax.rem(me + k, count)
            pltpu.make_async_remote_copy(
                block(peer), dst.at[me], out_seq.at[stage], in_seq.at[stage],
                device_id={"seq": peer_of(peer)}, device_id_type=MESH,
            ).start()
            return carry

        lax.fori_loop(1, count, step, 0)

    def sent(dst, stage, count):
        arrived(dst.at[pl.ds(0, count - 1)], out_seq.at[stage])

    project(1)
    pl.semaphore_wait(barrier, seqs + res - 2)
    send_head(1, rk, t, out_k, in_k, True)
    project(0)
    send_head(0, rq, z, out_q, in_q, False)
    project(2)

    @pl.when(jnp.logical_not(worker))
    def _():
        send_head(2, rv, t, out_v, in_v, True)

    one = lax.broadcasted_iota(jnp.int32, (tokens, tokens), 0)
    two = lax.broadcasted_iota(jnp.int32, (tokens, tokens), 1)
    turn = jnp.where((one % rows) * cols + one // rows == two, 1.0, 0.0).astype(bf16)
    back = jnp.where((two % rows) * cols + two // rows == one, 1.0, 0.0).astype(bf16)
    turned = jnp.dot(turn, x_ref[...].reshape(tokens, features), preferred_element_type=f32)
    xs[...] = turned.astype(bf16).reshape(seqs, per_device, rows, features)

    @pl.when(worker)
    def _():
        arrived(rk, in_k)
        arrived(rq, in_q)
        queries = jnp.concatenate([rq[:, r].reshape(here, LANES) for r in range(quads)], axis=1)
        keys = jnp.concatenate([rk[:, r].reshape(everywhere, LANES) for r in range(quads)], axis=1)
        logits = lax.dot_general(
            queries, keys, (((1,), (1,)), ((), ())), preferred_element_type=f32
        ) * (1.0 / (math.sqrt(HEAD) * math.sqrt(rows * seqs)))
        lp[...] = logits.astype(bf16).reshape(n_a, here // n_a, everywhere)
        exchange(lambda peer: lp.at[peer], rl, 0, a, n_a, a_peer)
        send_head(2, rv, t, out_v, in_v, True, FAR_FIRST[:2])
        arrived(rl, in_seq.at[0])
        total = jnp.sum(rl[...].astype(f32), axis=0)
        l2[...] = total.reshape(n_b, here // seqs, everywhere)
        exchange(lambda peer: l2.at[peer], r2, 1, b, n_b, b_peer)
        send_head(2, rv, t, out_v, in_v, True, FAR_FIRST[2:4])
        arrived(r2, in_seq.at[1])
        total = jnp.sum(r2[...], axis=0)
        total = jnp.exp(total - jnp.max(total, axis=-1, keepdims=True))
        total = total / jnp.sum(total, axis=-1, keepdims=True)
        td[...] = jnp.concatenate([total[:, :here], total[:, here:]], axis=0).astype(bf16)
        exchange(lambda peer: td, rd, 2, b, n_b, b_peer)
        send_head(2, rv, t, out_v, in_v, True, FAR_FIRST[4:6])
        arrived(rd, in_seq.at[2])
        tied = rd[...].astype(f32)
        tied = jnp.concatenate([tied[:, : here // seqs], tied[:, here // seqs :]], axis=2)
        t4[...] = tied.reshape(here // n_a, everywhere).astype(bf16)
        exchange(lambda peer: t4, rt, 3, a, n_a, a_peer)
        send_head(2, rv, t, out_v, in_v, True, FAR_FIRST[6:])
        arrived(rv, in_v)
        values = jnp.concatenate([rv[:, r].reshape(everywhere, LANES) for r in range(quads)], axis=1)
        arrived(rt, in_seq.at[3])
        context = jnp.dot(rt[...].reshape(here, everywhere), values, preferred_element_type=f32)
        for r in range(quads):
            oc[:, r] = context[:, r * LANES : (r + 1) * LANES].reshape(Z, cols, LANES).astype(bf16)
        for offset in FAR_FIRST:
            peer = lax.rem(z + offset, Z)
            if offset == 0:
                pltpu.make_async_copy(oc.at[z], rc.at[head_here], in_c).start()
            else:
                pltpu.make_async_remote_copy(
                    oc.at[peer], rc.at[head_here], out_c, in_c,
                    device_id={"res": yh * Z + peer}, device_id_type=MESH,
                ).start()

    exchange(lambda peer: xs.at[peer], rx, 4, s, seqs, s_peer)
    arrived(rc, in_c)
    low = low_lanes((half, LANES))
    tops, bottoms = [], []
    for pair in range(HEADS // 2):
        first = rc[2 * pair].reshape(half, LANES).astype(f32)
        second = rc[2 * pair + 1].reshape(half, LANES).astype(f32)
        tops.append(jnp.where(low, first, pltpu.roll(second, HEAD, 1)).astype(bf16))
        bottoms.append(jnp.where(low, pltpu.roll(first, HEAD, 1), second).astype(bf16))
    context = jnp.concatenate(
        [jnp.concatenate(tops, axis=1), jnp.concatenate(bottoms, axis=1)], axis=0
    )
    turned = jnp.dot(turn, context, preferred_element_type=f32)
    cs[...] = turned.astype(bf16).reshape(seqs, per_device, rows, INNER)
    exchange(lambda peer: cs.at[peer], rcs, 5, s, seqs, s_peer)
    loads[2].wait()
    loads[3].wait()

    update = jnp.dot(context, wo_ref[...], preferred_element_type=f32)
    source = x_ref[...].reshape(tokens, features).astype(f32)
    ru_ref[...] = (source + update).astype(bf16).reshape(rows, cols, features)
    arrived(rx, in_seq.at[4])
    arrived(rcs, in_seq.at[5])

    total_rows = seqs * rows
    low = low_lanes((total_rows, LANES))
    zero = jnp.zeros((total_rows, LANES), bf16)
    for c in range(per_device):
        update = jnp.dot(rcs[:, c].reshape(total_rows, INNER), wo_ref[...], preferred_element_type=f32)
        updated = (rx[:, c].reshape(total_rows, features).astype(f32) + update).astype(bf16)
        normed = layer_norm(updated.astype(f32), g2_ref[...].reshape(1, features)).astype(bf16)
        packed = jnp.dot(normed, w2_ref[...], preferred_element_type=f32).astype(bf16)
        for pair in range(HEADS // 2):
            span = slice(pair * LANES, (pair + 1) * LANES)
            query, key, value = (
                packed[:, part * INNER + pair * LANES : part * INNER + (pair + 1) * LANES]
                for part in range(3)
            )
            mixed = []
            for mask in (low, jnp.logical_not(low)):
                scores = lax.dot_general(
                    jnp.where(mask, query, zero), key, (((1,), (1,)), ((), ())), preferred_element_type=f32
                ) * (1.0 / math.sqrt(HEAD))
                scores = jnp.exp(scores - jnp.max(scores, axis=-1, keepdims=True))
                weights = (scores / jnp.sum(scores, axis=-1, keepdims=True)).astype(bf16)
                mixed.append(jnp.dot(weights, value, preferred_element_type=f32))
            ac[:, c, :, span] = jnp.where(low, mixed[0], mixed[1]).astype(bf16).reshape(seqs, rows, LANES)
    exchange(lambda peer: ac.at[peer], ra, 6, s, seqs, s_peer)
    sent_head(1, out_k, True)
    sent_head(0, out_q, False)
    sent_head(2, out_v, True)

    @pl.when(worker)
    def _():
        sent(rl, 0, n_a)
        sent(r2, 1, n_b)
        sent(rd, 2, n_b)
        sent(rt, 3, n_a)
        arrived(oc.at[pl.ds(0, Z - 1)], out_c)

    sent(rx, 4, seqs)
    sent(rcs, 5, seqs)
    arrived(ra, in_seq.at[6])
    result = jnp.dot(back, ra[...].reshape(tokens, INNER), preferred_element_type=f32).astype(bf16)
    cc_ref[...] = result.reshape(rows, cols, INNER)
    sent(ra, 6, seqs)


def body(seqs, alignment, row_gain, row_project, row_output, column_gain, column_project):
    rows, cols, features = alignment.shape
    res = 2 * Z
    here = Z * cols
    everywhere = res * cols
    share = here // seqs
    per_device = cols // seqs
    n_b = min(4, seqs // CORES)
    n_a = seqs // n_b
    f32, bf16 = jnp.float32, jnp.bfloat16
    vmem = pl.BlockSpec(memory_space=pltpu.VMEM)
    hbm = pl.BlockSpec(memory_space=pl.ANY)
    head = (rows // 2, cols, LANES)
    dma = pltpu.SemaphoreType.DMA
    return pl.pallas_call(
        functools.partial(kernel, seqs),
        out_shape=(
            jax.ShapeDtypeStruct((rows, cols, features), bf16),
            jax.ShapeDtypeStruct((rows, cols, INNER), bf16),
        ),
        in_specs=[hbm, vmem, hbm, vmem, hbm, hbm],
        out_specs=(vmem, vmem),
        scratch_shapes=[
            pltpu.VMEM(alignment.shape, bf16),
            pltpu.VMEM(row_project.shape, bf16),
            pltpu.VMEM(row_output.shape, bf16),
            pltpu.VMEM(column_project.shape, bf16),
            pltpu.VMEM((3, HEADS) + head, bf16),
            pltpu.VMEM((Z,) + head, bf16),
            pltpu.VMEM((res,) + head, bf16),
            pltpu.VMEM((res,) + head, bf16),
            pltpu.VMEM((n_a, here // n_a, everywhere), bf16),
            pltpu.VMEM((n_a, here // n_a, everywhere), bf16),
            pltpu.VMEM((n_b, share, everywhere), f32),
            pltpu.VMEM((n_b, share, everywhere), f32),
            pltpu.VMEM((2 * share, here), bf16),
            pltpu.VMEM((n_b, 2 * share, here), bf16),
            pltpu.VMEM((here // n_a, everywhere), bf16),
            pltpu.VMEM((n_a, here // n_a, everywhere), bf16),
            pltpu.VMEM((Z,) + head, bf16),
            pltpu.VMEM((HEADS,) + head, bf16),
            pltpu.VMEM((seqs, per_device, rows, features), bf16),
            pltpu.VMEM((seqs, per_device, rows, features), bf16),
            pltpu.VMEM((seqs, per_device, rows, INNER), bf16),
            pltpu.VMEM((seqs, per_device, rows, INNER), bf16),
            pltpu.VMEM((seqs, per_device, rows, INNER), bf16),
            pltpu.VMEM((seqs, per_device, rows, INNER), bf16),
            dma((4,)),
            dma((HEADS, 1)),
            dma((HEADS, 2)),
            dma((HEADS, 2)),
            dma,
            dma,
            dma,
            dma,
            dma,
            dma((7,)),
            dma((7,)),
        ],
        compiler_params=pltpu.CompilerParams(
            collective_id=0, has_side_effects=True, vmem_limit_bytes=60 * 1024 * 1024
        ),
        name="msa_layer",
    )(
        alignment, row_gain, row_project, column_gain, row_output, column_project,
    )


def solution(mesh):
    placed = (P("seq", "res", None), P(), P(), P(), P(), P())
    return jax.shard_map(
        functools.partial(body, mesh.shape["seq"]),
        mesh=mesh,
        in_specs=placed,
        out_specs=(P("seq", "res", None), P("seq", "res", None)),
        check_vma=False,
    )
```

```python
import functools
import math

import jax
import jax.numpy as jnp
from jax import lax
from jax.experimental import pallas as pl
from jax.experimental.pallas import tpu as pltpu
from jax.sharding import PartitionSpec as P

HEADS = 6
HEAD = 64
INNER = HEADS * HEAD
LANES = 128
Z = 8
CORES = 2
FAR_FIRST = (4, 3, 5, 2, 6, 1, 7, 0)
MESH = pl.DeviceIdType.MESH


def layer_norm(values, gain):
    average = jnp.mean(values, axis=-1, keepdims=True)
    centred = values - average
    spread = jnp.mean(centred * centred, axis=-1, keepdims=True)
    return centred * lax.rsqrt(spread + 1e-05) * gain.astype(jnp.float32)


def low_lanes(shape):
    return lax.broadcasted_iota(jnp.int32, shape, len(shape) - 1) < HEAD


def arrived(ref, sem):
    pltpu.make_async_copy(ref, ref, sem).wait()


def kernel(
    seqs, x_hbm, g1_hbm, w1_hbm, g2_hbm, wo_hbm, w2_hbm, ru_ref, cc_ref,
    x_ref, g1_ref, w1_ref, g2_ref, wo_ref, w2_ref, tiles, rq, rk, rv, lp, rl, l2, r2, t4, rt, oc, rc,
    xs, rx, cs, rcs, ac, ra,
    load_sem, out_q, out_k, out_v, out_p, in_p, in_q, in_k, in_v, out_c, in_c, out_seq, in_seq,
):
    rows, cols, features = x_ref.shape
    tokens = rows * cols
    half = tokens // 2
    quads = rows // 2
    res = 2 * Z
    here = Z * cols
    everywhere = res * cols
    per_device = cols // seqs
    n_b = min(4, seqs // CORES)
    n_a = seqs // n_b
    f32, bf16 = jnp.float32, jnp.bfloat16

    s = lax.axis_index("seq")
    t = lax.axis_index("res")
    yh = t // Z
    z = t % Z
    worker = z % 4 != 3
    head_here = z - z // 4
    core = s % CORES
    b = (s // CORES) % n_b
    a = s // (CORES * n_b) * CORES + core

    def away(offset):
        return lax.rem(z + offset + core * (Z - 2 * offset), Z)

    def a_peer(k):
        return (k // CORES) * (CORES * n_b) + b * CORES + k % CORES

    def b_peer(k):
        return (a // CORES) * (CORES * n_b) + k * CORES + core

    def s_peer(k):
        return k

    loads = [
        pltpu.make_async_copy(src, dst, load_sem.at[i])
        for i, (src, dst) in enumerate(
            (
                (x_hbm, x_ref), (g1_hbm, g1_ref), (w1_hbm, w1_ref),
                (g2_hbm, g2_ref), (wo_hbm, wo_ref), (w2_hbm, w2_ref),
            )
        )
    ]
    for load in loads:
        load.start()

    barrier = pltpu.get_barrier_semaphore()

    def greet_seq(k, carry):
        pl.semaphore_signal(barrier, inc=1, device_id={"seq": lax.rem(s + k, seqs)}, device_id_type=MESH)
        return carry

    def greet_res(k, carry):
        pl.semaphore_signal(barrier, inc=1, device_id={"res": lax.rem(t + k, res)}, device_id_type=MESH)
        return carry

    lax.fori_loop(1, res, greet_res, 0)
    lax.fori_loop(1, seqs, greet_seq, 0)

    loads[0].wait()
    loads[1].wait()
    source = x_ref[...].reshape(tokens, features).astype(f32)
    normed = layer_norm(source, g1_ref[...].reshape(1, features)).astype(bf16)
    loads[2].wait()

    def project(part):
        packed = jnp.dot(normed, w1_ref[:, part * INNER : (part + 1) * INNER], preferred_element_type=f32)
        for pair in range(HEADS // 2):
            tile = packed[:, pair * LANES : (pair + 1) * LANES]
            turned = pltpu.roll(tile, HEAD, 1)
            low = low_lanes((half, LANES))
            first = jnp.where(low, tile[:half], turned[half:]).astype(bf16)
            second = jnp.where(low, turned[:half], tile[half:]).astype(bf16)
            tiles[part, 2 * pair] = first.reshape(quads, cols, LANES)
            tiles[part, 2 * pair + 1] = second.reshape(quads, cols, LANES)

    def send_head(part, dst, slot, send, recv, both, offsets=FAR_FIRST):
        for offset in offsets:
            at = away(offset)

            @pl.when(at % 4 != 3)
            def _():
                h = at - at // 4
                block = tiles.at[part, h]
                if offset == 0:
                    pltpu.make_async_copy(block, dst.at[slot], recv).start()
                else:
                    pltpu.make_async_remote_copy(
                        block, dst.at[slot], send.at[h, 0], recv,
                        device_id={"res": yh * Z + at}, device_id_type=MESH,
                    ).start()
                if both:
                    pltpu.make_async_remote_copy(
                        block, dst.at[slot], send.at[h, 1], recv,
                        device_id={"res": (1 - yh) * Z + at}, device_id_type=MESH,
                    ).start()

    def send_values(offsets):
        if offsets[0] == FAR_FIRST[0]:
            pass_values.wait_recv()
        send_head(2, rv, t, out_v.at[0], in_v, False, offsets)
        send_head(3, rv, (1 - yh) * Z + z, out_v.at[1], in_v, False, offsets)

    def sent_head(part, send, both):
        def step(h, carry):
            at = h + h // 3
            block = tiles.at[part, h]

            @pl.when(z != at)
            def _():
                arrived(block, send.at[h, 0])

            if both:
                arrived(block, send.at[h, 1])
            return carry

        lax.fori_loop(0, HEADS, step, 0)

    def exchange(block, dst, stage, me, count, peer_of):
        pltpu.make_async_copy(block(me), dst.at[me], in_seq.at[stage]).start()

        def step(k, carry):
            peer = lax.rem(me + k + core * (count - 2 * k), count)
            pltpu.make_async_remote_copy(
                block(peer), dst.at[me], out_seq.at[stage], in_seq.at[stage],
                device_id={"seq": peer_of(peer)}, device_id_type=MESH,
            ).start()
            return carry

        lax.fori_loop(1, count, step, 0)

    def sent(dst, stage, count):
        arrived(dst.at[pl.ds(0, count - 1)], out_seq.at[stage])

    project(1)
    pl.semaphore_wait(barrier, seqs + res - 2)
    send_head(1, rk, t, out_k, in_k, True)
    project(0)
    send_head(0, rq, z, out_q, in_q, False)
    project(2)

    pass_values = pltpu.make_async_remote_copy(
        tiles.at[2], tiles.at[3], out_p, in_p, device_id={"res": (1 - yh) * Z + z}, device_id_type=MESH
    )
    pass_values.start()

    @pl.when(jnp.logical_not(worker))
    def _():
        send_values(FAR_FIRST)

    one = lax.broadcasted_iota(jnp.int32, (tokens, tokens), 0)
    two = lax.broadcasted_iota(jnp.int32, (tokens, tokens), 1)
    turn = jnp.where((one % rows) * cols + one // rows == two, 1.0, 0.0).astype(bf16)
    back = jnp.where((two % rows) * cols + two // rows == one, 1.0, 0.0).astype(bf16)
    turned = jnp.dot(turn, x_ref[...].reshape(tokens, features), preferred_element_type=f32)
    xs[...] = turned.astype(bf16).reshape(seqs, per_device, rows, features)

    @pl.when(worker)
    def _():
        arrived(rk, in_k)
        arrived(rq, in_q)
        queries = jnp.concatenate([rq[:, r].reshape(here, LANES) for r in range(quads)], axis=1)
        keys = jnp.concatenate([rk[:, r].reshape(everywhere, LANES) for r in range(quads)], axis=1)
        logits = lax.dot_general(
            queries, keys, (((1,), (1,)), ((), ())), preferred_element_type=f32
        ) * (1.0 / (math.sqrt(HEAD) * math.sqrt(rows * seqs)))
        lp[...] = logits.astype(bf16).reshape(n_a, here // n_a, everywhere)
        exchange(lambda peer: lp.at[peer], rl, 0, a, n_a, a_peer)
        send_values(FAR_FIRST[:3])
        arrived(rl, in_seq.at[0])
        total = jnp.sum(rl[...].astype(f32), axis=0)
        l2[...] = total.astype(bf16)
        exchange(lambda peer: l2, r2, 1, b, n_b, b_peer)
        send_values(FAR_FIRST[3:6])
        arrived(r2, in_seq.at[1])
        total = jnp.sum(r2[...].astype(f32), axis=0)
        total = jnp.exp(total - jnp.max(total, axis=-1, keepdims=True))
        total = total / jnp.sum(total, axis=-1, keepdims=True)
        t4[...] = total.astype(bf16)
        exchange(lambda peer: t4, rt, 2, a, n_a, a_peer)
        send_values(FAR_FIRST[6:])
        arrived(rv, in_v)
        values = jnp.concatenate([rv[:, r].reshape(everywhere, LANES) for r in range(quads)], axis=1)
        arrived(rt, in_seq.at[2])
        context = jnp.dot(rt[...].reshape(here, everywhere), values, preferred_element_type=f32)
        for r in range(quads):
            oc[:, r] = context[:, r * LANES : (r + 1) * LANES].reshape(Z, cols, LANES).astype(bf16)
        for offset in FAR_FIRST:
            peer = away(offset)
            if offset == 0:
                pltpu.make_async_copy(oc.at[z], rc.at[head_here], in_c).start()
            else:
                pltpu.make_async_remote_copy(
                    oc.at[peer], rc.at[head_here], out_c, in_c,
                    device_id={"res": yh * Z + peer}, device_id_type=MESH,
                ).start()

    exchange(lambda peer: xs.at[peer], rx, 3, s, seqs, s_peer)
    arrived(rc, in_c)
    low = low_lanes((half, LANES))
    tops, bottoms = [], []
    for pair in range(HEADS // 2):
        first = rc[2 * pair].reshape(half, LANES).astype(f32)
        second = rc[2 * pair + 1].reshape(half, LANES).astype(f32)
        tops.append(jnp.where(low, first, pltpu.roll(second, HEAD, 1)).astype(bf16))
        bottoms.append(jnp.where(low, pltpu.roll(first, HEAD, 1), second).astype(bf16))
    context = jnp.concatenate(
        [jnp.concatenate(tops, axis=1), jnp.concatenate(bottoms, axis=1)], axis=0
    )
    turned = jnp.dot(turn, context, preferred_element_type=f32)
    cs[...] = turned.astype(bf16).reshape(seqs, per_device, rows, INNER)
    exchange(lambda peer: cs.at[peer], rcs, 4, s, seqs, s_peer)
    for load in loads[3:]:
        load.wait()

    update = jnp.dot(context, wo_ref[...], preferred_element_type=f32)
    source = x_ref[...].reshape(tokens, features).astype(f32)
    ru_ref[...] = (source + update).astype(bf16).reshape(rows, cols, features)
    arrived(rx, in_seq.at[3])
    arrived(rcs, in_seq.at[4])

    total_rows = seqs * rows
    low = low_lanes((total_rows, LANES))
    zero = jnp.zeros((total_rows, LANES), bf16)
    for c in range(per_device):
        update = jnp.dot(rcs[:, c].reshape(total_rows, INNER), wo_ref[...], preferred_element_type=f32)
        updated = (rx[:, c].reshape(total_rows, features).astype(f32) + update).astype(bf16)
        normed = layer_norm(updated.astype(f32), g2_ref[...].reshape(1, features)).astype(bf16)
        packed = jnp.dot(normed, w2_ref[...], preferred_element_type=f32).astype(bf16)
        for pair in range(HEADS // 2):
            span = slice(pair * LANES, (pair + 1) * LANES)
            query, key, value = (
                packed[:, part * INNER + pair * LANES : part * INNER + (pair + 1) * LANES]
                for part in range(3)
            )
            mixed = []
            for mask in (low, jnp.logical_not(low)):
                scores = lax.dot_general(
                    jnp.where(mask, query, zero), key, (((1,), (1,)), ((), ())), preferred_element_type=f32
                ) * (1.0 / math.sqrt(HEAD))
                scores = jnp.exp(scores - jnp.max(scores, axis=-1, keepdims=True))
                weights = (scores / jnp.sum(scores, axis=-1, keepdims=True)).astype(bf16)
                mixed.append(jnp.dot(weights, value, preferred_element_type=f32))
            ac[:, c, :, span] = jnp.where(low, mixed[0], mixed[1]).astype(bf16).reshape(seqs, rows, LANES)
    exchange(lambda peer: ac.at[peer], ra, 5, s, seqs, s_peer)
    sent_head(1, out_k, True)
    sent_head(0, out_q, False)
    sent_head(2, out_v.at[0], False)
    sent_head(3, out_v.at[1], False)
    pass_values.wait_send()

    @pl.when(worker)
    def _():
        sent(rl, 0, n_a)
        sent(r2, 1, n_b)
        sent(rt, 2, n_a)
        arrived(oc.at[pl.ds(0, Z - 1)], out_c)

    sent(rx, 3, seqs)
    sent(rcs, 4, seqs)
    arrived(ra, in_seq.at[5])
    result = jnp.dot(back, ra[...].reshape(tokens, INNER), preferred_element_type=f32).astype(bf16)
    cc_ref[...] = result.reshape(rows, cols, INNER)
    sent(ra, 5, seqs)


def body(seqs, alignment, row_gain, row_project, row_output, column_gain, column_project):
    rows, cols, features = alignment.shape
    res = 2 * Z
    here = Z * cols
    everywhere = res * cols
    per_device = cols // seqs
    n_b = min(4, seqs // CORES)
    n_a = seqs // n_b
    bf16 = jnp.bfloat16
    vmem = pl.BlockSpec(memory_space=pltpu.VMEM)
    far = functools.partial(pltpu.with_memory_space_constraint, memory_space=pltpu.HBM)
    hbm = pl.BlockSpec(memory_space=pltpu.HBM)
    head = (rows // 2, cols, LANES)
    dma = pltpu.SemaphoreType.DMA
    return pl.pallas_call(
        functools.partial(kernel, seqs),
        out_shape=(
            jax.ShapeDtypeStruct((rows, cols, features), bf16),
            jax.ShapeDtypeStruct((rows, cols, INNER), bf16),
        ),
        in_specs=[hbm] * 6,
        out_specs=(vmem, vmem),
        scratch_shapes=[
            *(
                pltpu.VMEM(operand.shape, bf16)
                for operand in (
                    alignment, row_gain, row_project, column_gain, row_output, column_project
                )
            ),
            pltpu.VMEM((4, HEADS) + head, bf16),
            pltpu.VMEM((Z,) + head, bf16),
            pltpu.VMEM((res,) + head, bf16),
            pltpu.VMEM((res,) + head, bf16),
            pltpu.VMEM((n_a, here // n_a, everywhere), bf16),
            pltpu.VMEM((n_a, here // n_a, everywhere), bf16),
            pltpu.VMEM((here // n_a, everywhere), bf16),
            pltpu.VMEM((n_b, here // n_a, everywhere), bf16),
            pltpu.VMEM((here // n_a, everywhere), bf16),
            pltpu.VMEM((n_a, here // n_a, everywhere), bf16),
            pltpu.VMEM((Z,) + head, bf16),
            pltpu.VMEM((HEADS,) + head, bf16),
            pltpu.VMEM((seqs, per_device, rows, features), bf16),
            pltpu.VMEM((seqs, per_device, rows, features), bf16),
            pltpu.VMEM((seqs, per_device, rows, INNER), bf16),
            pltpu.VMEM((seqs, per_device, rows, INNER), bf16),
            pltpu.VMEM((seqs, per_device, rows, INNER), bf16),
            pltpu.VMEM((seqs, per_device, rows, INNER), bf16),
            dma((6,)),
            dma((HEADS, 1)),
            dma((HEADS, 2)),
            dma((2, HEADS, 1)),
            dma,
            dma,
            dma,
            dma,
            dma,
            dma,
            dma,
            dma((6,)),
            dma((6,)),
        ],
        compiler_params=pltpu.CompilerParams(
            collective_id=0, has_side_effects=True, vmem_limit_bytes=40 * 1024 * 1024
        ),
        name="msa_layer",
    )(
        far(alignment), far(row_gain), far(row_project), far(column_gain), far(row_output), far(column_project),
    )


def solution(mesh):
    placed = (P("seq", "res", None), P(), P(), P(), P(), P())
    return jax.shard_map(
        functools.partial(body, mesh.shape["seq"]),
        mesh=mesh,
        in_specs=placed,
        out_specs=(P("seq", "res", None), P("seq", "res", None)),
        check_vma=False,
    )
```

```python
import functools
import math

import jax
import jax.numpy as jnp
from jax import lax
from jax.experimental import pallas as pl
from jax.experimental.pallas import tpu as pltpu
from jax.sharding import PartitionSpec as P

HEADS = 6
HEAD = 64
INNER = HEADS * HEAD
LANES = 128
Z = 8
CORES = 2
FAR_FIRST = (4, 3, 5, 2, 6, 1, 7, 0)
MESH = pl.DeviceIdType.MESH


def layer_norm(values, gain):
    average = jnp.mean(values, axis=-1, keepdims=True)
    centred = values - average
    spread = jnp.mean(centred * centred, axis=-1, keepdims=True)
    return centred * lax.rsqrt(spread + 1e-05) * gain.astype(jnp.float32)


def low_lanes(shape):
    return lax.broadcasted_iota(jnp.int32, shape, len(shape) - 1) < HEAD


def arrived(ref, sem):
    pltpu.make_async_copy(ref, ref, sem).wait()


def kernel(
    seqs, x_hbm, g1_hbm, w1_hbm, g2_hbm, wo_hbm, w2_hbm, ru_ref, cc_ref,
    x_ref, g1_ref, w1_ref, g2_ref, wo_ref, w2_ref, tiles, rq, rk, rv, lp, rl, l2, r2, t4, rt, oc, rc,
    xs, rx, cs, rcs, ac, ra,
    load_sem, out_q, out_k, out_v, out_p, in_p, in_q, in_k, in_v, out_c, in_c, out_t, in_t, out_seq, in_seq,
):
    rows, cols, features = x_ref.shape
    tokens = rows * cols
    half = tokens // 2
    quads = rows // 2
    res = 2 * Z
    here = Z * cols
    everywhere = res * cols
    per_device = cols // seqs
    n_b = min(4, seqs // CORES)
    n_a = seqs // n_b
    count_t = Z // n_a
    f32, bf16 = jnp.float32, jnp.bfloat16

    s = lax.axis_index("seq")
    t = lax.axis_index("res")
    yh = t // Z
    z = t % Z
    worker = z % 4 != 3
    head_here = z - z // 4
    core = s % CORES
    b = (s // CORES) % n_b
    a = s // (CORES * n_b) * CORES + core

    def away(offset):
        return lax.rem(z + offset + core * (Z - 2 * offset), Z)

    def a_peer(k):
        return (k // CORES) * (CORES * n_b) + b * CORES + k % CORES

    def b_peer(k):
        return (a // CORES) * (CORES * n_b) + k * CORES + core

    def s_peer(k):
        return k

    loads = [
        pltpu.make_async_copy(src, dst, load_sem.at[i])
        for i, (src, dst) in enumerate(
            (
                (x_hbm, x_ref), (g1_hbm, g1_ref), (w1_hbm, w1_ref),
                (g2_hbm, g2_ref), (wo_hbm, wo_ref), (w2_hbm, w2_ref),
            )
        )
    ]
    for load in loads:
        load.start()

    barrier = pltpu.get_barrier_semaphore()

    def greet_seq(k, carry):
        pl.semaphore_signal(barrier, inc=1, device_id={"seq": lax.rem(s + k, seqs)}, device_id_type=MESH)
        return carry

    def greet_res(k, carry):
        pl.semaphore_signal(barrier, inc=1, device_id={"res": lax.rem(t + k, res)}, device_id_type=MESH)
        return carry

    lax.fori_loop(1, res, greet_res, 0)
    lax.fori_loop(1, seqs, greet_seq, 0)

    loads[0].wait()
    loads[1].wait()
    source = x_ref[...].reshape(tokens, features).astype(f32)
    normed = layer_norm(source, g1_ref[...].reshape(1, features)).astype(bf16)
    loads[2].wait()

    def project(part):
        packed = jnp.dot(normed, w1_ref[:, part * INNER : (part + 1) * INNER], preferred_element_type=f32)
        for pair in range(HEADS // 2):
            tile = packed[:, pair * LANES : (pair + 1) * LANES]
            turned = pltpu.roll(tile, HEAD, 1)
            low = low_lanes((half, LANES))
            first = jnp.where(low, tile[:half], turned[half:]).astype(bf16)
            second = jnp.where(low, turned[:half], tile[half:]).astype(bf16)
            tiles[part, 2 * pair] = first.reshape(quads, cols, LANES)
            tiles[part, 2 * pair + 1] = second.reshape(quads, cols, LANES)

    def send_head(part, dst, slot, send, recv, both, offsets=FAR_FIRST):
        for offset in offsets:
            at = away(offset)

            @pl.when(at % 4 != 3)
            def _():
                h = at - at // 4
                block = tiles.at[part, h]
                if offset == 0:
                    pltpu.make_async_copy(block, dst.at[slot], recv).start()
                else:
                    pltpu.make_async_remote_copy(
                        block, dst.at[slot], send.at[h, 0], recv,
                        device_id={"res": yh * Z + at}, device_id_type=MESH,
                    ).start()
                if both:
                    pltpu.make_async_remote_copy(
                        block, dst.at[slot], send.at[h, 1], recv,
                        device_id={"res": (1 - yh) * Z + at}, device_id_type=MESH,
                    ).start()

    def send_values(offsets):
        if offsets[0] == FAR_FIRST[0]:
            pass_values.wait_recv()
        send_head(2, rv, t, out_v.at[0], in_v, False, offsets)
        send_head(3, rv, (1 - yh) * Z + z, out_v.at[1], in_v, False, offsets)

    def sent_head(part, send, both):
        def step(h, carry):
            at = h + h // 3
            block = tiles.at[part, h]

            @pl.when(z != at)
            def _():
                arrived(block, send.at[h, 0])

            if both:
                arrived(block, send.at[h, 1])
            return carry

        lax.fori_loop(0, HEADS, step, 0)

    def exchange(block, dst, stage, me, count, peer_of):
        pltpu.make_async_copy(block(me), dst.at[me], in_seq.at[stage]).start()

        def step(k, carry):
            peer = lax.rem(me + k + core * (count - 2 * k), count)
            pltpu.make_async_remote_copy(
                block(peer), dst.at[me], out_seq.at[stage], in_seq.at[stage],
                device_id={"seq": peer_of(peer)}, device_id_type=MESH,
            ).start()
            return carry

        lax.fori_loop(1, count, step, 0)

    def sent(dst, stage, count):
        arrived(dst.at[pl.ds(0, count - 1)], out_seq.at[stage])

    project(1)
    pl.semaphore_wait(barrier, seqs + res - 2)
    send_head(1, rk, t, out_k, in_k, True)
    project(0)
    send_head(0, rq, z, out_q, in_q.at[z], False)
    project(2)

    pass_values = pltpu.make_async_remote_copy(
        tiles.at[2], tiles.at[3], out_p, in_p, device_id={"res": (1 - yh) * Z + z}, device_id_type=MESH
    )
    pass_values.start()

    @pl.when(jnp.logical_not(worker))
    def _():
        send_values(FAR_FIRST)

    one = lax.broadcasted_iota(jnp.int32, (tokens, tokens), 0)
    two = lax.broadcasted_iota(jnp.int32, (tokens, tokens), 1)
    turn = jnp.where((one % rows) * cols + one // rows == two, 1.0, 0.0).astype(bf16)
    back = jnp.where((two % rows) * cols + two // rows == one, 1.0, 0.0).astype(bf16)
    turned = jnp.dot(turn, x_ref[...].reshape(tokens, features), preferred_element_type=f32)
    xs[...] = turned.astype(bf16).reshape(seqs, per_device, rows, features)

    @pl.when(worker)
    def _():
        arrived(rk, in_k)
        keys = jnp.concatenate([rk[:, r].reshape(everywhere, LANES) for r in range(quads)], axis=1)
        for offset in (4, 5, 3, 6, 2, 7, 1, 0):
            origin = away(offset)
            arrived(rq.at[origin], in_q.at[origin])
            queries = jnp.concatenate([rq[origin, r] for r in range(quads)], axis=1)
            logits = lax.dot_general(
                queries, keys, (((1,), (1,)), ((), ())), preferred_element_type=f32
            ) * (1.0 / (math.sqrt(HEAD) * math.sqrt(rows * seqs)))
            lp[origin] = logits.astype(bf16)
            owner = origin // count_t
            slot = rl.at[a, origin % count_t]

            @pl.when(owner == a)
            def _():
                pltpu.make_async_copy(lp.at[origin], slot, in_seq.at[0]).start()

            @pl.when(owner != a)
            def _():
                pltpu.make_async_remote_copy(
                    lp.at[origin], slot, out_seq.at[0], in_seq.at[0],
                    device_id={"seq": a_peer(owner)}, device_id_type=MESH,
                ).start()

        send_values(FAR_FIRST[:3])
        arrived(rl, in_seq.at[0])
        total = jnp.sum(rl[...].astype(f32), axis=0)
        l2[...] = total.astype(bf16)
        exchange(lambda peer: l2, r2, 1, b, n_b, b_peer)
        send_values(FAR_FIRST[3:6])
        arrived(r2, in_seq.at[1])
        total = jnp.sum(r2[...].astype(f32), axis=0)
        total = jnp.exp(total - jnp.max(total, axis=-1, keepdims=True))
        total = total / jnp.sum(total, axis=-1, keepdims=True)
        t4[...] = total.astype(bf16)
        for k in range(count_t):
            pltpu.make_async_copy(t4.at[k], rt.at[a * count_t + k], in_t.at[a * count_t + k]).start()

            def step(n, carry, k=k):
                peer = lax.rem(a + n + core * (n_a - 2 * n), n_a)
                pltpu.make_async_remote_copy(
                    t4.at[k], rt.at[a * count_t + k], out_t, in_t.at[a * count_t + k],
                    device_id={"seq": a_peer(peer)}, device_id_type=MESH,
                ).start()
                return carry

            lax.fori_loop(1, n_a, step, 0)
        send_values(FAR_FIRST[6:])
        arrived(rv, in_v)
        values = jnp.concatenate([rv[:, r].reshape(everywhere, LANES) for r in range(quads)], axis=1)
        for offset in FAR_FIRST:
            peer = away(offset)
            arrived(rt.at[peer], in_t.at[peer])
            context = jnp.dot(rt[peer], values, preferred_element_type=f32).astype(bf16)
            for r in range(quads):
                oc[peer, r] = context[:, r * LANES : (r + 1) * LANES]
            if offset == 0:
                pltpu.make_async_copy(oc.at[z], rc.at[head_here], in_c).start()
            else:
                pltpu.make_async_remote_copy(
                    oc.at[peer], rc.at[head_here], out_c, in_c,
                    device_id={"res": yh * Z + peer}, device_id_type=MESH,
                ).start()

    exchange(lambda peer: xs.at[peer], rx, 3, s, seqs, s_peer)
    arrived(rc, in_c)
    low = low_lanes((half, LANES))
    tops, bottoms = [], []
    for pair in range(HEADS // 2):
        first = rc[2 * pair].reshape(half, LANES).astype(f32)
        second = rc[2 * pair + 1].reshape(half, LANES).astype(f32)
        tops.append(jnp.where(low, first, pltpu.roll(second, HEAD, 1)).astype(bf16))
        bottoms.append(jnp.where(low, pltpu.roll(first, HEAD, 1), second).astype(bf16))
    context = jnp.concatenate(
        [jnp.concatenate(tops, axis=1), jnp.concatenate(bottoms, axis=1)], axis=0
    )
    turned = jnp.dot(turn, context, preferred_element_type=f32)
    cs[...] = turned.astype(bf16).reshape(seqs, per_device, rows, INNER)
    exchange(lambda peer: cs.at[peer], rcs, 4, s, seqs, s_peer)
    for load in loads[3:]:
        load.wait()

    update = jnp.dot(context, wo_ref[...], preferred_element_type=f32)
    source = x_ref[...].reshape(tokens, features).astype(f32)
    ru_ref[...] = (source + update).astype(bf16).reshape(rows, cols, features)
    arrived(rx, in_seq.at[3])
    arrived(rcs, in_seq.at[4])

    total_rows = seqs * rows
    parts = 2
    some = total_rows // parts
    low = low_lanes((some, LANES))
    zero = jnp.zeros((some, LANES), bf16)
    columns = []
    for c in range(per_device):
        update = jnp.dot(rcs[:, c].reshape(total_rows, INNER), wo_ref[...], preferred_element_type=f32)
        updated = (rx[:, c].reshape(total_rows, features).astype(f32) + update).astype(bf16)
        normed = layer_norm(updated.astype(f32), g2_ref[...].reshape(1, features)).astype(bf16)
        columns.append(jnp.dot(normed, w2_ref[...], preferred_element_type=f32).astype(bf16))
    for part in range(parts):
        peers = seqs // parts
        for c, packed in enumerate(columns):
            for pair in range(HEADS // 2):
                span = slice(pair * LANES, (pair + 1) * LANES)
                query = packed[part * some : (part + 1) * some, span]
                key = packed[:, INNER + pair * LANES : INNER + (pair + 1) * LANES]
                value = packed[:, 2 * INNER + pair * LANES : 2 * INNER + (pair + 1) * LANES]
                mixed = []
                for mask in (low, jnp.logical_not(low)):
                    scores = lax.dot_general(
                        jnp.where(mask, query, zero), key, (((1,), (1,)), ((), ())), preferred_element_type=f32
                    ) * (1.0 / math.sqrt(HEAD))
                    scores = jnp.exp(scores - jnp.max(scores, axis=-1, keepdims=True))
                    weights = (scores / jnp.sum(scores, axis=-1, keepdims=True)).astype(bf16)
                    mixed.append(jnp.dot(weights, value, preferred_element_type=f32))
                ac[part * peers : (part + 1) * peers, c, :, span] = (
                    jnp.where(low, mixed[0], mixed[1]).astype(bf16).reshape(peers, rows, LANES)
                )

        def step(k, carry, part=part, peers=peers):
            peer = part * peers + lax.rem(s + k, peers)

            @pl.when(peer == s)
            def _():
                pltpu.make_async_copy(ac.at[s], ra.at[s], in_seq.at[5]).start()

            @pl.when(peer != s)
            def _():
                pltpu.make_async_remote_copy(
                    ac.at[peer], ra.at[s], out_seq.at[5], in_seq.at[5],
                    device_id={"seq": peer}, device_id_type=MESH,
                ).start()

            return carry

        lax.fori_loop(0, peers, step, 0)
    sent_head(1, out_k, True)
    sent_head(0, out_q, False)
    sent_head(2, out_v.at[0], False)
    sent_head(3, out_v.at[1], False)
    pass_values.wait_send()

    @pl.when(worker)
    def _():
        arrived(lp.at[pl.ds(0, Z - count_t)], out_seq.at[0])
        sent(r2, 1, n_b)
        arrived(rt.at[pl.ds(0, Z - count_t)], out_t)
        arrived(oc.at[pl.ds(0, Z - 1)], out_c)

    sent(rx, 3, seqs)
    sent(rcs, 4, seqs)
    arrived(ra, in_seq.at[5])
    result = jnp.dot(back, ra[...].reshape(tokens, INNER), preferred_element_type=f32).astype(bf16)
    cc_ref[...] = result.reshape(rows, cols, INNER)
    sent(ra, 5, seqs)


def body(seqs, alignment, row_gain, row_project, row_output, column_gain, column_project):
    rows, cols, features = alignment.shape
    res = 2 * Z
    here = Z * cols
    everywhere = res * cols
    per_device = cols // seqs
    n_b = min(4, seqs // CORES)
    n_a = seqs // n_b
    bf16 = jnp.bfloat16
    vmem = pl.BlockSpec(memory_space=pltpu.VMEM)
    far = functools.partial(pltpu.with_memory_space_constraint, memory_space=pltpu.HBM)
    hbm = pl.BlockSpec(memory_space=pltpu.HBM)
    head = (rows // 2, cols, LANES)
    dma = pltpu.SemaphoreType.DMA
    return pl.pallas_call(
        functools.partial(kernel, seqs),
        out_shape=(
            jax.ShapeDtypeStruct((rows, cols, features), bf16),
            jax.ShapeDtypeStruct((rows, cols, INNER), bf16),
        ),
        in_specs=[hbm] * 6,
        out_specs=(vmem, vmem),
        scratch_shapes=[
            *(
                pltpu.VMEM(operand.shape, bf16)
                for operand in (
                    alignment, row_gain, row_project, column_gain, row_output, column_project
                )
            ),
            pltpu.VMEM((4, HEADS) + head, bf16),
            pltpu.VMEM((Z,) + head, bf16),
            pltpu.VMEM((res,) + head, bf16),
            pltpu.VMEM((res,) + head, bf16),
            pltpu.VMEM((Z, cols, everywhere), bf16),
            pltpu.VMEM((n_a, Z // n_a, cols, everywhere), bf16),
            pltpu.VMEM((Z // n_a, cols, everywhere), bf16),
            pltpu.VMEM((n_b, Z // n_a, cols, everywhere), bf16),
            pltpu.VMEM((Z // n_a, cols, everywhere), bf16),
            pltpu.VMEM((Z, cols, everywhere), bf16),
            pltpu.VMEM((Z,) + head, bf16),
            pltpu.VMEM((HEADS,) + head, bf16),
            pltpu.VMEM((seqs, per_device, rows, features), bf16),
            pltpu.VMEM((seqs, per_device, rows, features), bf16),
            pltpu.VMEM((seqs, per_device, rows, INNER), bf16),
            pltpu.VMEM((seqs, per_device, rows, INNER), bf16),
            pltpu.VMEM((seqs, per_device, rows, INNER), bf16),
            pltpu.VMEM((seqs, per_device, rows, INNER), bf16),
            dma((6,)),
            dma((HEADS, 1)),
            dma((HEADS, 2)),
            dma((2, HEADS, 1)),
            dma,
            dma,
            dma((Z,)),
            dma,
            dma,
            dma,
            dma,
            dma,
            dma((Z,)),
            dma((6,)),
            dma((6,)),
        ],
        compiler_params=pltpu.CompilerParams(
            collective_id=0, has_side_effects=True, vmem_limit_bytes=40 * 1024 * 1024
        ),
        name="msa_layer",
    )(
        far(alignment), far(row_gain), far(row_project), far(column_gain), far(row_output), far(column_project),
    )


def solution(mesh):
    placed = (P("seq", "res", None), P(), P(), P(), P(), P())
    return jax.shard_map(
        functools.partial(body, mesh.shape["seq"]),
        mesh=mesh,
        in_specs=placed,
        out_specs=(P("seq", "res", None), P("seq", "res", None)),
        check_vma=False,
    )
```

```python
import functools
import math

import jax
import jax.numpy as jnp
from jax import lax
from jax.experimental import pallas as pl
from jax.experimental.pallas import tpu as pltpu
from jax.sharding import PartitionSpec as P

HEADS = 6
HEAD = 64
INNER = HEADS * HEAD
LANES = 128
Z = 8
CORES = 2
FAR_FIRST = (4, 3, 5, 2, 6, 1, 7, 0)
MESH = pl.DeviceIdType.MESH


def layer_norm(values, gain):
    average = jnp.mean(values, axis=-1, keepdims=True)
    centred = values - average
    spread = jnp.mean(centred * centred, axis=-1, keepdims=True)
    return centred * lax.rsqrt(spread + 1e-05) * gain.astype(jnp.float32)


def flipped(index, k, count):
    both, bit = 0, 1
    while bit < count:
        both += ((index // bit) % 2) * ((k // bit) % 2) * bit
        bit *= 2
    return index + k - 2 * both


def low_lanes(shape):
    return lax.broadcasted_iota(jnp.int32, shape, len(shape) - 1) < HEAD


def arrived(ref, sem):
    pltpu.make_async_copy(ref, ref, sem).wait()


def kernel(
    seqs, x_hbm, g1_hbm, w1_hbm, g2_hbm, wo_hbm, w2_hbm, ru_ref, cc_ref,
    x_ref, g1_ref, w1_ref, g2_ref, wo_ref, w2_ref, tiles, rq, rk, rv, lp, rl, l2, r2, t4, rt, oc, rc,
    xs, rx, cs, rcs, ac, ra,
    load_sem, out_q, out_k, out_v, out_p, in_p, in_q, in_k, in_v, out_c, in_c, out_t, in_t, out_seq, in_seq,
):
    rows, cols, features = x_ref.shape
    tokens = rows * cols
    half = tokens // 2
    quads = rows // 2
    res = 2 * Z
    here = Z * cols
    everywhere = res * cols
    per_device = cols // seqs
    n_b = min(4, seqs // CORES)
    n_a = seqs // n_b
    count_t = Z // n_a
    f32, bf16 = jnp.float32, jnp.bfloat16

    s = lax.axis_index("seq")
    t = lax.axis_index("res")
    yh = t // Z
    z = t % Z
    worker = z % 4 != 3
    head_here = z - z // 4
    core = s % CORES
    b = (s // CORES) % n_b
    a = s // (CORES * n_b) * CORES + core

    def away(offset):
        return lax.rem(z + offset + core * (Z - 2 * offset), Z)

    def a_peer(k):
        return (k // CORES) * (CORES * n_b) + b * CORES + k % CORES

    def b_peer(k):
        return (a // CORES) * (CORES * n_b) + k * CORES + core

    def s_peer(k):
        return k

    loads = [
        pltpu.make_async_copy(src, dst, load_sem.at[i])
        for i, (src, dst) in enumerate(
            (
                (x_hbm, x_ref), (g1_hbm, g1_ref), (w1_hbm, w1_ref),
                (g2_hbm, g2_ref), (wo_hbm, wo_ref), (w2_hbm, w2_ref),
            )
        )
    ]
    for load in loads:
        load.start()

    barrier = pltpu.get_barrier_semaphore()

    def greet_seq(k, carry):
        pl.semaphore_signal(barrier, inc=1, device_id={"seq": lax.rem(s + k, seqs)}, device_id_type=MESH)
        return carry

    def greet_res(k, carry):
        pl.semaphore_signal(barrier, inc=1, device_id={"res": lax.rem(t + k, res)}, device_id_type=MESH)
        return carry

    lax.fori_loop(1, res, greet_res, 0)
    lax.fori_loop(1, seqs, greet_seq, 0)

    loads[0].wait()
    loads[1].wait()
    source = x_ref[...].reshape(tokens, features).astype(f32)
    normed = layer_norm(source, g1_ref[...].reshape(1, features)).astype(bf16)
    loads[2].wait()

    def project(part):
        packed = jnp.dot(normed, w1_ref[:, part * INNER : (part + 1) * INNER], preferred_element_type=f32)
        for pair in range(HEADS // 2):
            tile = packed[:, pair * LANES : (pair + 1) * LANES]
            turned = pltpu.roll(tile, HEAD, 1)
            low = low_lanes((half, LANES))
            first = jnp.where(low, tile[:half], turned[half:]).astype(bf16)
            second = jnp.where(low, turned[:half], tile[half:]).astype(bf16)
            tiles[part, 2 * pair] = first.reshape(quads, cols, LANES)
            tiles[part, 2 * pair + 1] = second.reshape(quads, cols, LANES)

    def send_head(part, dst, slot, send, recv, both, offsets=FAR_FIRST):
        for offset in offsets:
            at = away(offset)

            @pl.when(at % 4 != 3)
            def _():
                h = at - at // 4
                block = tiles.at[part, h]
                if offset == 0:
                    pltpu.make_async_copy(block, dst.at[slot], recv).start()
                else:
                    pltpu.make_async_remote_copy(
                        block, dst.at[slot], send.at[h, 0], recv,
                        device_id={"res": yh * Z + at}, device_id_type=MESH,
                    ).start()
                if both:
                    pltpu.make_async_remote_copy(
                        block, dst.at[slot], send.at[h, 1], recv,
                        device_id={"res": (1 - yh) * Z + at}, device_id_type=MESH,
                    ).start()

    def send_values(offsets):
        if offsets[0] == FAR_FIRST[0]:
            pass_values.wait_recv()
        send_head(2, rv, t, out_v.at[0], in_v, False, offsets)
        send_head(3, rv, (1 - yh) * Z + z, out_v.at[1], in_v, False, offsets)

    def sent_head(part, send, both):
        def step(h, carry):
            at = h + h // 3
            block = tiles.at[part, h]

            @pl.when(z != at)
            def _():
                arrived(block, send.at[h, 0])

            if both:
                arrived(block, send.at[h, 1])
            return carry

        lax.fori_loop(0, HEADS, step, 0)

    def exchange(block, dst, stage, me, count, peer_of):
        pltpu.make_async_copy(block(me), dst.at[me], in_seq.at[stage]).start()

        def step(k, carry):
            peer = flipped(me, count - k, count)
            pltpu.make_async_remote_copy(
                block(peer), dst.at[me], out_seq.at[stage], in_seq.at[stage],
                device_id={"seq": peer_of(peer)}, device_id_type=MESH,
            ).start()
            return carry

        lax.fori_loop(1, count, step, 0)

    def sent(dst, stage, count):
        arrived(dst.at[pl.ds(0, count - 1)], out_seq.at[stage])

    project(1)
    pl.semaphore_wait(barrier, seqs + res - 2)
    send_head(1, rk, t, out_k, in_k, True)
    project(0)
    send_head(0, rq, z, out_q, in_q.at[z], False)
    project(2)

    pass_values = pltpu.make_async_remote_copy(
        tiles.at[2], tiles.at[3], out_p, in_p, device_id={"res": (1 - yh) * Z + z}, device_id_type=MESH
    )
    pass_values.start()

    @pl.when(jnp.logical_not(worker))
    def _():
        send_values(FAR_FIRST)

    one = lax.broadcasted_iota(jnp.int32, (tokens, tokens), 0)
    two = lax.broadcasted_iota(jnp.int32, (tokens, tokens), 1)
    turn = jnp.where((one % rows) * cols + one // rows == two, 1.0, 0.0).astype(bf16)
    back = jnp.where((two % rows) * cols + two // rows == one, 1.0, 0.0).astype(bf16)
    turned = jnp.dot(turn, x_ref[...].reshape(tokens, features), preferred_element_type=f32)
    xs[...] = turned.astype(bf16).reshape(seqs, per_device, rows, features)

    @pl.when(worker)
    def _():
        arrived(rk, in_k)
        keys = jnp.concatenate([rk[:, r].reshape(everywhere, LANES) for r in range(quads)], axis=1)
        for offset in (4, 5, 3, 6, 2, 7, 1, 0):
            origin = away(offset)
            arrived(rq.at[origin], in_q.at[origin])
            queries = jnp.concatenate([rq[origin, r] for r in range(quads)], axis=1)
            logits = lax.dot_general(
                queries, keys, (((1,), (1,)), ((), ())), preferred_element_type=f32
            ) * (1.0 / (math.sqrt(HEAD) * math.sqrt(rows * seqs)))
            lp[origin] = logits.astype(bf16)
            owner = origin // count_t
            slot = rl.at[a, origin % count_t]

            @pl.when(owner == a)
            def _():
                pltpu.make_async_copy(lp.at[origin], slot, in_seq.at[0]).start()

            @pl.when(owner != a)
            def _():
                pltpu.make_async_remote_copy(
                    lp.at[origin], slot, out_seq.at[0], in_seq.at[0],
                    device_id={"seq": a_peer(owner)}, device_id_type=MESH,
                ).start()

        send_values(FAR_FIRST[:3])
        arrived(rl, in_seq.at[0])
        total = jnp.sum(rl[...].astype(f32), axis=0)
        l2[...] = total.astype(bf16)
        exchange(lambda peer: l2, r2, 1, b, n_b, b_peer)
        send_values(FAR_FIRST[3:6])
        arrived(r2, in_seq.at[1])
        total = jnp.sum(r2[...].astype(f32), axis=0)
        total = jnp.exp(total - jnp.max(total, axis=-1, keepdims=True))
        total = total / jnp.sum(total, axis=-1, keepdims=True)
        t4[...] = total.astype(bf16)
        for k in range(count_t):
            pltpu.make_async_copy(t4.at[k], rt.at[a * count_t + k], in_t.at[a * count_t + k]).start()

            def step(n, carry, k=k):
                peer = flipped(a, n_a - n, n_a)
                pltpu.make_async_remote_copy(
                    t4.at[k], rt.at[a * count_t + k], out_t, in_t.at[a * count_t + k],
                    device_id={"seq": a_peer(peer)}, device_id_type=MESH,
                ).start()
                return carry

            lax.fori_loop(1, n_a, step, 0)
        send_values(FAR_FIRST[6:])
        arrived(rv, in_v)
        values = jnp.concatenate([rv[:, r].reshape(everywhere, LANES) for r in range(quads)], axis=1)
        for offset in FAR_FIRST:
            peer = away(offset)
            arrived(rt.at[peer], in_t.at[peer])
            context = jnp.dot(rt[peer], values, preferred_element_type=f32).astype(bf16)
            for r in range(quads):
                oc[peer, r] = context[:, r * LANES : (r + 1) * LANES]
            if offset == 0:
                pltpu.make_async_copy(oc.at[z], rc.at[head_here], in_c).start()
            else:
                pltpu.make_async_remote_copy(
                    oc.at[peer], rc.at[head_here], out_c, in_c,
                    device_id={"res": yh * Z + peer}, device_id_type=MESH,
                ).start()

    exchange(lambda peer: xs.at[peer], rx, 3, s, seqs, s_peer)
    arrived(rc, in_c)
    low = low_lanes((half, LANES))
    tops, bottoms = [], []
    for pair in range(HEADS // 2):
        first = rc[2 * pair].reshape(half, LANES).astype(f32)
        second = rc[2 * pair + 1].reshape(half, LANES).astype(f32)
        tops.append(jnp.where(low, first, pltpu.roll(second, HEAD, 1)).astype(bf16))
        bottoms.append(jnp.where(low, pltpu.roll(first, HEAD, 1), second).astype(bf16))
    context = jnp.concatenate(
        [jnp.concatenate(tops, axis=1), jnp.concatenate(bottoms, axis=1)], axis=0
    )
    turned = jnp.dot(turn, context, preferred_element_type=f32)
    cs[...] = turned.astype(bf16).reshape(seqs, per_device, rows, INNER)
    exchange(lambda peer: cs.at[peer], rcs, 4, s, seqs, s_peer)
    for load in loads[3:]:
        load.wait()

    update = jnp.dot(context, wo_ref[...], preferred_element_type=f32)
    source = x_ref[...].reshape(tokens, features).astype(f32)
    ru_ref[...] = (source + update).astype(bf16).reshape(rows, cols, features)
    arrived(rx, in_seq.at[3])
    arrived(rcs, in_seq.at[4])

    total_rows = seqs * rows
    parts = 2
    some = total_rows // parts
    low = low_lanes((some, LANES))
    zero = jnp.zeros((some, LANES), bf16)
    columns = []
    for c in range(per_device):
        update = jnp.dot(rcs[:, c].reshape(total_rows, INNER), wo_ref[...], preferred_element_type=f32)
        updated = (rx[:, c].reshape(total_rows, features).astype(f32) + update).astype(bf16)
        normed = layer_norm(updated.astype(f32), g2_ref[...].reshape(1, features)).astype(bf16)
        columns.append(jnp.dot(normed, w2_ref[...], preferred_element_type=f32).astype(bf16))
    for part in range(parts):
        peers = seqs // parts
        for c, packed in enumerate(columns):
            for pair in range(HEADS // 2):
                span = slice(pair * LANES, (pair + 1) * LANES)
                query = packed[part * some : (part + 1) * some, span]
                key = packed[:, INNER + pair * LANES : INNER + (pair + 1) * LANES]
                value = packed[:, 2 * INNER + pair * LANES : 2 * INNER + (pair + 1) * LANES]
                mixed = []
                for mask in (low, jnp.logical_not(low)):
                    scores = lax.dot_general(
                        jnp.where(mask, query, zero), key, (((1,), (1,)), ((), ())), preferred_element_type=f32
                    ) * (1.0 / math.sqrt(HEAD))
                    scores = jnp.exp(scores - jnp.max(scores, axis=-1, keepdims=True))
                    weights = (scores / jnp.sum(scores, axis=-1, keepdims=True)).astype(bf16)
                    mixed.append(jnp.dot(weights, value, preferred_element_type=f32))
                ac[part * peers : (part + 1) * peers, c, :, span] = (
                    jnp.where(low, mixed[0], mixed[1]).astype(bf16).reshape(peers, rows, LANES)
                )

        def step(k, carry, part=part, peers=peers):
            peer = part * peers + flipped(s % peers, peers - 1 - k, peers)

            @pl.when(peer == s)
            def _():
                pltpu.make_async_copy(ac.at[s], ra.at[s], in_seq.at[5]).start()

            @pl.when(peer != s)
            def _():
                pltpu.make_async_remote_copy(
                    ac.at[peer], ra.at[s], out_seq.at[5], in_seq.at[5],
                    device_id={"seq": peer}, device_id_type=MESH,
                ).start()

            return carry

        lax.fori_loop(0, peers, step, 0)
    sent_head(1, out_k, True)
    sent_head(0, out_q, False)
    sent_head(2, out_v.at[0], False)
    sent_head(3, out_v.at[1], False)
    pass_values.wait_send()

    @pl.when(worker)
    def _():
        arrived(lp.at[pl.ds(0, Z - count_t)], out_seq.at[0])
        sent(r2, 1, n_b)
        arrived(rt.at[pl.ds(0, Z - count_t)], out_t)
        arrived(oc.at[pl.ds(0, Z - 1)], out_c)

    sent(rx, 3, seqs)
    sent(rcs, 4, seqs)
    arrived(ra, in_seq.at[5])
    result = jnp.dot(back, ra[...].reshape(tokens, INNER), preferred_element_type=f32).astype(bf16)
    cc_ref[...] = result.reshape(rows, cols, INNER)
    sent(ra, 5, seqs)


def body(seqs, alignment, row_gain, row_project, row_output, column_gain, column_project):
    rows, cols, features = alignment.shape
    res = 2 * Z
    here = Z * cols
    everywhere = res * cols
    per_device = cols // seqs
    n_b = min(4, seqs // CORES)
    n_a = seqs // n_b
    bf16 = jnp.bfloat16
    vmem = pl.BlockSpec(memory_space=pltpu.VMEM)
    far = functools.partial(pltpu.with_memory_space_constraint, memory_space=pltpu.HBM)
    hbm = pl.BlockSpec(memory_space=pltpu.HBM)
    head = (rows // 2, cols, LANES)
    dma = pltpu.SemaphoreType.DMA
    return pl.pallas_call(
        functools.partial(kernel, seqs),
        out_shape=(
            jax.ShapeDtypeStruct((rows, cols, features), bf16),
            jax.ShapeDtypeStruct((rows, cols, INNER), bf16),
        ),
        in_specs=[hbm] * 6,
        out_specs=(vmem, vmem),
        scratch_shapes=[
            *(
                pltpu.VMEM(operand.shape, bf16)
                for operand in (
                    alignment, row_gain, row_project, column_gain, row_output, column_project
                )
            ),
            pltpu.VMEM((4, HEADS) + head, bf16),
            pltpu.VMEM((Z,) + head, bf16),
            pltpu.VMEM((res,) + head, bf16),
            pltpu.VMEM((res,) + head, bf16),
            pltpu.VMEM((Z, cols, everywhere), bf16),
            pltpu.VMEM((n_a, Z // n_a, cols, everywhere), bf16),
            pltpu.VMEM((Z // n_a, cols, everywhere), bf16),
            pltpu.VMEM((n_b, Z // n_a, cols, everywhere), bf16),
            pltpu.VMEM((Z // n_a, cols, everywhere), bf16),
            pltpu.VMEM((Z, cols, everywhere), bf16),
            pltpu.VMEM((Z,) + head, bf16),
            pltpu.VMEM((HEADS,) + head, bf16),
            pltpu.VMEM((seqs, per_device, rows, features), bf16),
            pltpu.VMEM((seqs, per_device, rows, features), bf16),
            pltpu.VMEM((seqs, per_device, rows, INNER), bf16),
            pltpu.VMEM((seqs, per_device, rows, INNER), bf16),
            pltpu.VMEM((seqs, per_device, rows, INNER), bf16),
            pltpu.VMEM((seqs, per_device, rows, INNER), bf16),
            dma((6,)),
            dma((HEADS, 1)),
            dma((HEADS, 2)),
            dma((2, HEADS, 1)),
            dma,
            dma,
            dma((Z,)),
            dma,
            dma,
            dma,
            dma,
            dma,
            dma((Z,)),
            dma((6,)),
            dma((6,)),
        ],
        compiler_params=pltpu.CompilerParams(
            collective_id=0, has_side_effects=True, vmem_limit_bytes=40 * 1024 * 1024
        ),
        name="msa_layer",
    )(
        far(alignment), far(row_gain), far(row_project), far(column_gain), far(row_output), far(column_project),
    )


def solution(mesh):
    placed = (P("seq", "res", None), P(), P(), P(), P(), P())
    return jax.shard_map(
        functools.partial(body, mesh.shape["seq"]),
        mesh=mesh,
        in_specs=placed,
        out_specs=(P("seq", "res", None), P("seq", "res", None)),
        check_vma=False,
    )
```

```python
import functools
import math

import jax
import jax.numpy as jnp
from jax import lax
from jax.experimental import pallas as pl
from jax.experimental.pallas import tpu as pltpu
from jax.sharding import PartitionSpec as P

HEADS = 6
HEAD = 64
INNER = HEADS * HEAD
LANES = 128
Z = 8
CORES = 2
FAR_FIRST = (4, 3, 5, 2, 6, 1, 7, 0)
MESH = pl.DeviceIdType.MESH


def layer_norm(values, gain):
    average = jnp.mean(values, axis=-1, keepdims=True)
    centred = values - average
    spread = jnp.mean(centred * centred, axis=-1, keepdims=True)
    return centred * lax.rsqrt(spread + 1e-05) * gain.astype(jnp.float32)


def flipped(index, k, count):
    both, bit = 0, 1
    while bit < count:
        both += ((index // bit) % 2) * ((k // bit) % 2) * bit
        bit *= 2
    return index + k - 2 * both


def low_lanes(shape):
    return lax.broadcasted_iota(jnp.int32, shape, len(shape) - 1) < HEAD


def arrived(ref, sem):
    pltpu.make_async_copy(ref, ref, sem).wait()


def kernel(
    seqs, x_hbm, g1_hbm, w1_hbm, g2_hbm, wo_hbm, w2_hbm, ru_ref, cc_ref,
    x_ref, g1_ref, w1_ref, g2_ref, wo_ref, w2_ref, tiles, rq, rk, rv, lp, rl, l2, r2, t4, rt, oc, rc,
    xs, rx, cs, rcs, ac, ra,
    load_sem, out_q, out_k, out_v, out_p, in_p, in_q, in_k, in_v, out_c, in_c, out_t, in_t, out_seq, in_seq,
):
    rows, cols, features = x_ref.shape
    tokens = rows * cols
    half = tokens // 2
    quads = rows // 2
    res = 2 * Z
    here = Z * cols
    everywhere = res * cols
    per_device = cols // seqs
    n_b = min(4, seqs // CORES)
    n_a = seqs // n_b
    count_t = Z // n_a
    f32, bf16 = jnp.float32, jnp.bfloat16

    s = lax.axis_index("seq")
    t = lax.axis_index("res")
    yh = t // Z
    z = t % Z
    worker = z % 4 != 3
    head_here = z - z // 4
    core = s % CORES
    b = (s // CORES) % n_b
    a = s // (CORES * n_b) * CORES + core

    def away(offset):
        return lax.rem(z + offset + core * (Z - 2 * offset), Z)

    def a_peer(k):
        return (k // CORES) * (CORES * n_b) + b * CORES + k % CORES

    def b_peer(k):
        return (a // CORES) * (CORES * n_b) + k * CORES + core

    def s_peer(k):
        return k

    loads = [
        pltpu.make_async_copy(src, dst, load_sem.at[i])
        for i, (src, dst) in enumerate(
            (
                (x_hbm, x_ref), (g1_hbm, g1_ref), (w1_hbm, w1_ref),
                (g2_hbm, g2_ref), (wo_hbm, wo_ref), (w2_hbm, w2_ref),
            )
        )
    ]
    for load in loads:
        load.start()

    barrier = pltpu.get_barrier_semaphore()

    def greet_seq(k, carry):
        pl.semaphore_signal(barrier, inc=1, device_id={"seq": lax.rem(s + k, seqs)}, device_id_type=MESH)
        return carry

    def greet_res(k, carry):
        pl.semaphore_signal(barrier, inc=1, device_id={"res": lax.rem(t + k, res)}, device_id_type=MESH)
        return carry

    lax.fori_loop(1, res, greet_res, 0)
    lax.fori_loop(1, seqs, greet_seq, 0)

    loads[0].wait()
    loads[1].wait()
    source = x_ref[...].reshape(tokens, features).astype(f32)
    normed = layer_norm(source, g1_ref[...].reshape(1, features)).astype(bf16)
    loads[2].wait()

    def project(part):
        packed = jnp.dot(normed, w1_ref[:, part * INNER : (part + 1) * INNER], preferred_element_type=f32)
        for pair in range(HEADS // 2):
            tile = packed[:, pair * LANES : (pair + 1) * LANES]
            turned = pltpu.roll(tile, HEAD, 1)
            low = low_lanes((half, LANES))
            first = jnp.where(low, tile[:half], turned[half:]).astype(bf16)
            second = jnp.where(low, turned[:half], tile[half:]).astype(bf16)
            tiles[part, 2 * pair] = first.reshape(quads, cols, LANES)
            tiles[part, 2 * pair + 1] = second.reshape(quads, cols, LANES)

    def send_head(part, dst, slot, send, recv, both, offsets=FAR_FIRST):
        for offset in offsets:
            at = away(offset)

            @pl.when(at % 4 != 3)
            def _():
                h = at - at // 4
                block = tiles.at[part, h]
                if offset == 0:
                    pltpu.make_async_copy(block, dst.at[slot], recv).start()
                else:
                    pltpu.make_async_remote_copy(
                        block, dst.at[slot], send.at[h, 0], recv,
                        device_id={"res": yh * Z + at}, device_id_type=MESH,
                    ).start()
                if both:
                    pltpu.make_async_remote_copy(
                        block, dst.at[slot], send.at[h, 1], recv,
                        device_id={"res": (1 - yh) * Z + at}, device_id_type=MESH,
                    ).start()

    def send_values(offsets):
        if offsets[0] == FAR_FIRST[0]:
            pass_values.wait_recv()
        send_head(2, rv, t, out_v.at[0], in_v, False, offsets)
        send_head(3, rv, (1 - yh) * Z + z, out_v.at[1], in_v, False, offsets)

    def sent_head(part, send, both):
        def step(h, carry):
            at = h + h // 3
            block = tiles.at[part, h]

            @pl.when(z != at)
            def _():
                arrived(block, send.at[h, 0])

            if both:
                arrived(block, send.at[h, 1])
            return carry

        lax.fori_loop(0, HEADS, step, 0)

    def exchange(block, dst, stage, me, count, peer_of):
        pltpu.make_async_copy(block(me), dst.at[me], in_seq.at[stage]).start()

        def step(k, carry):
            peer = flipped(me, count - k, count)
            pltpu.make_async_remote_copy(
                block(peer), dst.at[me], out_seq.at[stage], in_seq.at[stage],
                device_id={"seq": peer_of(peer)}, device_id_type=MESH,
            ).start()
            return carry

        lax.fori_loop(1, count, step, 0)

    def sent(dst, stage, count):
        arrived(dst.at[pl.ds(0, count - 1)], out_seq.at[stage])

    project(1)
    pl.semaphore_wait(barrier, seqs + res - 2)
    send_head(1, rk, t, out_k, in_k, True)
    project(0)
    send_head(0, rq, z, out_q, in_q.at[z], False)
    project(2)

    pass_values = pltpu.make_async_remote_copy(
        tiles.at[2], tiles.at[3], out_p, in_p, device_id={"res": (1 - yh) * Z + z}, device_id_type=MESH
    )
    pass_values.start()

    @pl.when(jnp.logical_not(worker))
    def _():
        send_values(FAR_FIRST)

    one = lax.broadcasted_iota(jnp.int32, (tokens, tokens), 0)
    two = lax.broadcasted_iota(jnp.int32, (tokens, tokens), 1)
    turn = jnp.where((one % rows) * cols + one // rows == two, 1.0, 0.0).astype(bf16)
    back = jnp.where((two % rows) * cols + two // rows == one, 1.0, 0.0).astype(bf16)
    turned = jnp.dot(turn, x_ref[...].reshape(tokens, features), preferred_element_type=f32)
    xs[...] = turned.astype(bf16).reshape(seqs, per_device, rows, features)

    @pl.when(worker)
    def _():
        arrived(rk, in_k)
        keys = jnp.concatenate([rk[:, r].reshape(everywhere, LANES) for r in range(quads)], axis=1)
        for offset in (4, 5, 3, 6, 2, 7, 1, 0):
            origin = away(offset)
            arrived(rq.at[origin], in_q.at[origin])
            queries = jnp.concatenate([rq[origin, r] for r in range(quads)], axis=1)
            logits = lax.dot_general(
                queries, keys, (((1,), (1,)), ((), ())), preferred_element_type=f32
            ) * (1.0 / (math.sqrt(HEAD) * math.sqrt(rows * seqs)))
            lp[origin] = logits.astype(bf16)
            owner = origin // count_t
            slot = rl.at[a, origin % count_t]

            @pl.when(owner == a)
            def _():
                pltpu.make_async_copy(lp.at[origin], slot, in_seq.at[0]).start()

            @pl.when(owner != a)
            def _():
                pltpu.make_async_remote_copy(
                    lp.at[origin], slot, out_seq.at[0], in_seq.at[0],
                    device_id={"seq": a_peer(owner)}, device_id_type=MESH,
                ).start()

        send_values(FAR_FIRST[:3])
        arrived(rl, in_seq.at[0])
        total = jnp.sum(rl[...].astype(f32), axis=0)
        l2[...] = total.astype(bf16)
        exchange(lambda peer: l2, r2, 1, b, n_b, b_peer)
        send_values(FAR_FIRST[3:6])
        arrived(r2, in_seq.at[1])
        total = jnp.sum(r2[...].astype(f32), axis=0)
        total = jnp.exp(total - jnp.max(total, axis=-1, keepdims=True))
        total = total / jnp.sum(total, axis=-1, keepdims=True)
        t4[...] = total.astype(bf16)
        for k in range(count_t):
            pltpu.make_async_copy(t4.at[k], rt.at[a * count_t + k], in_t.at[a * count_t + k]).start()

            def step(n, carry, k=k):
                peer = flipped(a, n_a - n, n_a)
                pltpu.make_async_remote_copy(
                    t4.at[k], rt.at[a * count_t + k], out_t, in_t.at[a * count_t + k],
                    device_id={"seq": a_peer(peer)}, device_id_type=MESH,
                ).start()
                return carry

            lax.fori_loop(1, n_a, step, 0)
        send_values(FAR_FIRST[6:])
        arrived(rv, in_v)
        values = jnp.concatenate([rv[:, r].reshape(everywhere, LANES) for r in range(quads)], axis=1)
        for group in (FAR_FIRST[:4], FAR_FIRST[4:]):
            homes = [away(offset) for offset in group]
            for home in homes:
                arrived(rt.at[home], in_t.at[home])
            tied = jnp.concatenate([rt[home] for home in homes], axis=0)
            context = jnp.dot(tied, values, preferred_element_type=f32).astype(bf16)
            for n, (offset, home) in enumerate(zip(group, homes)):
                for r in range(quads):
                    oc[home, r] = context[n * cols : (n + 1) * cols, r * LANES : (r + 1) * LANES]
                if offset == 0:
                    pltpu.make_async_copy(oc.at[z], rc.at[head_here], in_c).start()
                else:
                    pltpu.make_async_remote_copy(
                        oc.at[home], rc.at[head_here], out_c, in_c,
                        device_id={"res": yh * Z + home}, device_id_type=MESH,
                    ).start()

    exchange(lambda peer: xs.at[peer], rx, 3, s, seqs, s_peer)
    arrived(rc, in_c)
    low = low_lanes((half, LANES))
    tops, bottoms = [], []
    for pair in range(HEADS // 2):
        first = rc[2 * pair].reshape(half, LANES).astype(f32)
        second = rc[2 * pair + 1].reshape(half, LANES).astype(f32)
        tops.append(jnp.where(low, first, pltpu.roll(second, HEAD, 1)).astype(bf16))
        bottoms.append(jnp.where(low, pltpu.roll(first, HEAD, 1), second).astype(bf16))
    context = jnp.concatenate(
        [jnp.concatenate(tops, axis=1), jnp.concatenate(bottoms, axis=1)], axis=0
    )
    turned = jnp.dot(turn, context, preferred_element_type=f32)
    cs[...] = turned.astype(bf16).reshape(seqs, per_device, rows, INNER)
    exchange(lambda peer: cs.at[peer], rcs, 4, s, seqs, s_peer)
    for load in loads[3:]:
        load.wait()

    update = jnp.dot(context, wo_ref[...], preferred_element_type=f32)
    source = x_ref[...].reshape(tokens, features).astype(f32)
    ru_ref[...] = (source + update).astype(bf16).reshape(rows, cols, features)
    arrived(rx, in_seq.at[3])
    arrived(rcs, in_seq.at[4])

    total_rows = seqs * rows
    parts = 2
    some = total_rows // parts
    low = low_lanes((some, LANES))
    zero = jnp.zeros((some, LANES), bf16)
    columns = []
    for c in range(per_device):
        update = jnp.dot(rcs[:, c].reshape(total_rows, INNER), wo_ref[...], preferred_element_type=f32)
        updated = (rx[:, c].reshape(total_rows, features).astype(f32) + update).astype(bf16)
        normed = layer_norm(updated.astype(f32), g2_ref[...].reshape(1, features)).astype(bf16)
        columns.append(jnp.dot(normed, w2_ref[...], preferred_element_type=f32).astype(bf16))
    for part in range(parts):
        peers = seqs // parts
        for c, packed in enumerate(columns):
            for pair in range(HEADS // 2):
                span = slice(pair * LANES, (pair + 1) * LANES)
                query = packed[part * some : (part + 1) * some, span]
                key = packed[:, INNER + pair * LANES : INNER + (pair + 1) * LANES]
                value = packed[:, 2 * INNER + pair * LANES : 2 * INNER + (pair + 1) * LANES]
                mixed = []
                for mask in (low, jnp.logical_not(low)):
                    scores = lax.dot_general(
                        jnp.where(mask, query, zero), key, (((1,), (1,)), ((), ())), preferred_element_type=f32
                    ) * (1.0 / math.sqrt(HEAD))
                    scores = jnp.exp(scores - jnp.max(scores, axis=-1, keepdims=True))
                    weights = (scores / jnp.sum(scores, axis=-1, keepdims=True)).astype(bf16)
                    mixed.append(jnp.dot(weights, value, preferred_element_type=f32))
                ac[part * peers : (part + 1) * peers, c, :, span] = (
                    jnp.where(low, mixed[0], mixed[1]).astype(bf16).reshape(peers, rows, LANES)
                )

        def step(k, carry, part=part, peers=peers):
            peer = part * peers + flipped(s % peers, peers - 1 - k, peers)

            @pl.when(peer == s)
            def _():
                pltpu.make_async_copy(ac.at[s], ra.at[s], in_seq.at[5]).start()

            @pl.when(peer != s)
            def _():
                pltpu.make_async_remote_copy(
                    ac.at[peer], ra.at[s], out_seq.at[5], in_seq.at[5],
                    device_id={"seq": peer}, device_id_type=MESH,
                ).start()

            return carry

        lax.fori_loop(0, peers, step, 0)
    sent_head(1, out_k, True)
    sent_head(0, out_q, False)
    sent_head(2, out_v.at[0], False)
    sent_head(3, out_v.at[1], False)
    pass_values.wait_send()

    @pl.when(worker)
    def _():
        arrived(lp.at[pl.ds(0, Z - count_t)], out_seq.at[0])
        sent(r2, 1, n_b)
        arrived(rt.at[pl.ds(0, Z - count_t)], out_t)
        arrived(oc.at[pl.ds(0, Z - 1)], out_c)

    sent(rx, 3, seqs)
    sent(rcs, 4, seqs)
    arrived(ra, in_seq.at[5])
    result = jnp.dot(back, ra[...].reshape(tokens, INNER), preferred_element_type=f32).astype(bf16)
    cc_ref[...] = result.reshape(rows, cols, INNER)
    sent(ra, 5, seqs)


def body(seqs, alignment, row_gain, row_project, row_output, column_gain, column_project):
    rows, cols, features = alignment.shape
    res = 2 * Z
    here = Z * cols
    everywhere = res * cols
    per_device = cols // seqs
    n_b = min(4, seqs // CORES)
    n_a = seqs // n_b
    bf16 = jnp.bfloat16
    vmem = pl.BlockSpec(memory_space=pltpu.VMEM)
    far = functools.partial(pltpu.with_memory_space_constraint, memory_space=pltpu.HBM)
    hbm = pl.BlockSpec(memory_space=pltpu.HBM)
    head = (rows // 2, cols, LANES)
    dma = pltpu.SemaphoreType.DMA
    return pl.pallas_call(
        functools.partial(kernel, seqs),
        out_shape=(
            jax.ShapeDtypeStruct((rows, cols, features), bf16),
            jax.ShapeDtypeStruct((rows, cols, INNER), bf16),
        ),
        in_specs=[hbm] * 6,
        out_specs=(vmem, vmem),
        scratch_shapes=[
            *(
                pltpu.VMEM(operand.shape, bf16)
                for operand in (
                    alignment, row_gain, row_project, column_gain, row_output, column_project
                )
            ),
            pltpu.VMEM((4, HEADS) + head, bf16),
            pltpu.VMEM((Z,) + head, bf16),
            pltpu.VMEM((res,) + head, bf16),
            pltpu.VMEM((res,) + head, bf16),
            pltpu.VMEM((Z, cols, everywhere), bf16),
            pltpu.VMEM((n_a, Z // n_a, cols, everywhere), bf16),
            pltpu.VMEM((Z // n_a, cols, everywhere), bf16),
            pltpu.VMEM((n_b, Z // n_a, cols, everywhere), bf16),
            pltpu.VMEM((Z // n_a, cols, everywhere), bf16),
            pltpu.VMEM((Z, cols, everywhere), bf16),
            pltpu.VMEM((Z,) + head, bf16),
            pltpu.VMEM((HEADS,) + head, bf16),
            pltpu.VMEM((seqs, per_device, rows, features), bf16),
            pltpu.VMEM((seqs, per_device, rows, features), bf16),
            pltpu.VMEM((seqs, per_device, rows, INNER), bf16),
            pltpu.VMEM((seqs, per_device, rows, INNER), bf16),
            pltpu.VMEM((seqs, per_device, rows, INNER), bf16),
            pltpu.VMEM((seqs, per_device, rows, INNER), bf16),
            dma((6,)),
            dma((HEADS, 1)),
            dma((HEADS, 2)),
            dma((2, HEADS, 1)),
            dma,
            dma,
            dma((Z,)),
            dma,
            dma,
            dma,
            dma,
            dma,
            dma((Z,)),
            dma((6,)),
            dma((6,)),
        ],
        compiler_params=pltpu.CompilerParams(
            collective_id=0, has_side_effects=True, vmem_limit_bytes=40 * 1024 * 1024
        ),
        name="msa_layer",
    )(
        far(alignment), far(row_gain), far(row_project), far(column_gain), far(row_output), far(column_project),
    )


def solution(mesh):
    placed = (P("seq", "res", None), P(), P(), P(), P(), P())
    return jax.shard_map(
        functools.partial(body, mesh.shape["seq"]),
        mesh=mesh,
        in_specs=placed,
        out_specs=(P("seq", "res", None), P("seq", "res", None)),
        check_vma=False,
    )
```
